32 devices in a mesh: depth: 16 (over z, x, core), azi: 2 (over y).
Axes of the slice: x: 2, y: 2, z: 4, core: 2. Of those that a mesh axis runs over, the one named last changes fastest.
Arguments:
- heat_state: float32 [256, 128, 1024], P('depth', None, 'azi'), may hold values from -6 to 6
- tangent_in: float32 [256, 128, 1024], P('depth', None, 'azi'), may hold values from -6 to 6
- cotangent: float32 [256, 128, 1024], P('depth', None, 'azi'), may hold values from -6 to 6
- wet_mask: int32 [256, 1024], P('depth', 'azi'), may hold values 0 or 1
- sensors: int32 [256, 1024], P('depth', 'azi'), may hold values from 0 to 127
- propagators: bfloat16 [1024, 128, 128], P('azi', 'depth'), as said below
Outputs:
- new_state: bfloat16 [256, 128, 1024], P('depth', None, 'azi')
- tangent_out: bfloat16 [256, 128, 1024], P('depth', None, 'azi')
- gradient: float32 [256, 128, 1024], P('depth', None, 'azi')
- readings: bfloat16 [256, 1024], P('depth', 'azi')
The draws below stay inside these ranges and needn't reach their ends.
Inputs may be any that keep to these rules, and one draw needn't show every extreme that they name: `propagators`: each mode's radial propagator has diagonal entries between 0.55 and 1 and off-diagonal entries of magnitude at most 1.4 / sqrt(128).
All inputs are finite; a program needn't handle non-finite values. No bound on the sum of `wet_mask` on one device may be relied on, other than what follows from the above.
Results may differ from the reference program's by a relative error of at most 0.0078.
Values may be sent and summed in bfloat16 or wider, within the bound.
A program may use at most 128 MiB of HBM per device.

```python
import math
import jax
import jax.numpy as jnp
from jax import lax

A = 1024
R = 128
Z = 256


def draw_propagators(key, part):
    diag_key = jax.random.fold_in(key, 11)
    off_key = jax.random.fold_in(key, 23)
    diagonal = jax.random.uniform(diag_key, (A, R, 1), jnp.float32, 0.55, 1.0)
    spread = 0.35 / R ** 0.5
    off_diag = jnp.clip(jax.random.normal(off_key, (A, R, R), jnp.float32), -4.0, 4.0) * spread
    row_index = jnp.arange(R, dtype=jnp.int32)[None, :, None]
    col_index = jnp.arange(R, dtype=jnp.int32)[None, None, :]
    return jnp.where(row_index == col_index, diagonal, off_diag).astype(jnp.bfloat16)


def place_ends(values, key, least, top_value):
    extent = values.shape
    index_at = [jax.random.randint(jax.random.fold_in(key, axis), (), 0, extent[axis]) for axis in range(len(extent))]
    values = values.at[tuple(index_at)].set(least)
    longest = extent.index(max(extent))
    index_at[longest] = (index_at[longest] + 1) % extent[longest]
    return values.at[tuple(index_at)].set(top_value)


def levels(own_key, extent, pieces, least, high):
    def one(axis_at, parts):
        heights = jax.random.uniform(jax.random.fold_in(jax.random.fold_in(own_key, 6), axis_at), (parts,), jnp.float32, least / len(pieces), high / len(pieces))
        return jnp.repeat(jnp.exp(heights), extent[axis_at] // parts).reshape((-1,) + (1,) * (len(extent) - axis_at - 1))

    level = one(*pieces[0])
    for cut in pieces[1:]:
        level = level * one(*cut)
    return level


def bell_draw(own_key, shape, scale, bound, cuts=(), held_as=jnp.bfloat16):
    entries = jax.random.normal(own_key, shape, jnp.float32) * scale
    if len(cuts) > 0:
        entries = levels(own_key, shape, cuts, -0.22, 0.18) * entries
    return jnp.clip(entries, min=-bound, max=bound).astype(held_as)


def setup_inputs(seed: int = 0) -> dict:
    seeds = jax.random.split(jax.random.key(seed), 7)
    heat_state = bell_draw(seeds[0], (Z, R, A), 1.0, 6.0, ((0, 16), (2, 2)), jnp.float32)
    tangent_in = bell_draw(seeds[1], (Z, R, A), 1.0, 6.0, ((0, 16), (2, 2)), jnp.float32)
    cotangent = bell_draw(seeds[2], (Z, R, A), 1.0, 6.0, ((0, 16), (2, 2)), jnp.float32)
    wet_mask = place_ends((jax.random.randint(seeds[3], (Z, A), 0, 2) < 1).astype(jnp.int32), jax.random.fold_in(seeds[3], 1), 0, 1)
    sensors = place_ends(jax.random.randint(seeds[4], (Z, A), 0, R), jax.random.fold_in(seeds[4], 1), 0, R - 1).astype(jnp.int32)
    propagators = draw_propagators(jax.random.fold_in(seeds[6], 71), 0)
    return {"heat_state": heat_state, "tangent_in": tangent_in, "cotangent": cotangent, "wet_mask": wet_mask, "sensors": sensors, "propagators": propagators}


mixing = 0.25
evaporation = 0.6
skin_depth = 16.0

def fourier_table(length):
    wavenumber = jnp.arange(length, dtype=jnp.int32)[:, None]
    position = jnp.arange(length, dtype=jnp.int32)[None, :]
    midpoint = length // 2
    harmonic = jnp.where(wavenumber <= midpoint, wavenumber, wavenumber - midpoint)
    phase_angle = (harmonic * position % length).astype(jnp.float32) * (2.0 * math.pi / length)
    waveform = jnp.where(wavenumber <= midpoint, jnp.cos(phase_angle), jnp.sin(phase_angle))
    boundary_rows = (wavenumber == 0) | (wavenumber == midpoint)
    weights = jnp.where(boundary_rows, math.sqrt(1.0 / length), math.sqrt(2.0 / length))
    return (waveform * weights).astype(jnp.bfloat16)

def depth_mix(field):
    padded = jnp.pad(field, ((1, 1), (0, 0), (0, 0)))
    return padded[2:] + padded[:-2] - 2.0 * field

def reference(heat_state, tangent_in, cotangent, wet_mask, sensors, propagators):
    fourier = fourier_table(A).astype(jnp.float32)
    prop_full = propagators.astype(jnp.float32)
    profile = jnp.exp(-jnp.arange(R).astype(jnp.float32) / skin_depth)[None, :, None]
    damping = evaporation * wet_mask.astype(jnp.float32)[:, None, :] * profile
    moisture = jnp.tanh(heat_state)
    slope = 1.0 - moisture * moisture
    forward_rhs = (heat_state + mixing * depth_mix(heat_state) - damping * moisture).astype(jnp.bfloat16)
    tangent_rhs = (tangent_in + mixing * depth_mix(tangent_in) - damping * slope * tangent_in).astype(jnp.bfloat16)
    adjoint_seed = cotangent.astype(jnp.bfloat16)
    block = math.gcd(Z, 8)
    highest = lax.Precision.HIGHEST

    def spectral(fields, flipped):
        grouped = fields.reshape(Z // block, block, R, A)

        def one_block(piece):
            spectrum = jnp.einsum('ka,zra->zrk', fourier, piece.astype(jnp.float32), precision=highest).astype(jnp.bfloat16)
            if flipped:
                solved = jnp.einsum('ksr,zsk->zrk', prop_full, spectrum.astype(jnp.float32), precision=highest)
            else:
                solved = jnp.einsum('krs,zsk->zrk', prop_full, spectrum.astype(jnp.float32), precision=highest)
            solved = solved.astype(jnp.bfloat16)
            return jnp.einsum('ka,zrk->zra', fourier, solved.astype(jnp.float32), precision=highest).astype(jnp.bfloat16)
        return lax.map(one_block, grouped).reshape(Z, R, A)
    new_state = spectral(forward_rhs, False)
    tangent_out = spectral(tangent_rhs, False)
    dual = spectral(adjoint_seed, True).astype(jnp.float32)
    gradient = dual + mixing * depth_mix(dual) - damping * slope * dual
    readings = jnp.take_along_axis(new_state, sensors[:, None, :].astype(jnp.int32), axis=1)[:, 0, :]
    return (new_state, tangent_out, gradient, readings)
```

```python
import math

import jax
import jax.numpy as jnp
import numpy as np
from jax import lax
from jax.experimental import pallas as pl
from jax.sharding import PartitionSpec as P

mixing = 0.25
evaporation = 0.6
skin_depth = 16.0


def halo_planes(last, first):
    size = lax.axis_size("depth")
    up = [(i, i + 1) for i in range(size - 1)]
    down = [(j, i) for i, j in up]
    before = lax.ppermute(last, "depth", up)
    after = lax.ppermute(first, "depth", down)
    return before, after


def damping_profile(rows, lanes):
    radius = pl.program_id(0) * rows + lax.broadcasted_iota(jnp.int32, (rows, lanes), 0)
    return evaporation * jnp.exp(-radius.astype(jnp.float32) / skin_depth)


def plane(ref, before, after, z):
    source, index = (before, 0) if z < 0 else (after, 0) if z == ref.shape[0] else (ref, z)
    return source[index].astype(jnp.float32)


def mixed(ref, before, after, z):
    centre = plane(ref, before, after, z)
    around = plane(ref, before, after, z + 1) + plane(ref, before, after, z - 1)
    return centre, centre + mixing * (around - 2.0 * centre)


def rhs_kernel(wet, heat, heat_before, heat_after, tangent, tangent_before, tangent_after, out, tangent_out):
    slab, rows, lanes = heat.shape
    profile = damping_profile(rows, lanes)
    for z in range(slab):
        damping = wet[z : z + 1].astype(jnp.float32) * profile
        centre, value = mixed(heat, heat_before, heat_after, z)
        moisture = jnp.tanh(centre)
        out[z] = (value - damping * moisture).astype(out.dtype)
        slope = 1.0 - moisture * moisture
        centre, value = mixed(tangent, tangent_before, tangent_after, z)
        tangent_out[z] = (value - damping * slope * centre).astype(tangent_out.dtype)


def gradient_kernel(wet, heat, dual, dual_before, dual_after, out):
    slab, rows, lanes = heat.shape
    profile = damping_profile(rows, lanes)
    for z in range(slab):
        damping = wet[z : z + 1].astype(jnp.float32) * profile
        moisture = jnp.tanh(heat[z])
        slope = 1.0 - moisture * moisture
        centre, value = mixed(dual, dual_before, dual_after, z)
        out[z] = value - damping * slope * centre


def by_radius(kernel, wet, fields, dtypes):
    slab, radial, lanes = fields[0].shape
    rows = min(radial, 16)

    def spec(depth):
        return pl.BlockSpec((depth, rows, lanes), lambda i: (0, i, 0))

    count = len(dtypes) * slab * radial * lanes
    return pl.pallas_call(
        kernel,
        grid=(radial // rows,),
        in_specs=[pl.BlockSpec(wet.shape, lambda i: (0, 0))] + [spec(f.shape[0]) for f in fields],
        out_specs=[spec(slab) for _ in dtypes],
        out_shape=[jax.ShapeDtypeStruct((slab, radial, lanes), dtype) for dtype in dtypes],
        cost_estimate=pl.CostEstimate(flops=10 * count, bytes_accessed=6 * count, transcendentals=count),
    )(wet, *fields)


def fourier_table(length):
    wavenumber = np.arange(length, dtype=np.int32)[:, None]
    position = np.arange(length, dtype=np.int32)[None, :]
    midpoint = length // 2
    harmonic = np.where(wavenumber <= midpoint, wavenumber, wavenumber - midpoint)
    phase = (harmonic * position % length).astype(np.float32) * np.float32(2.0 * math.pi / length)
    waveform = np.where(wavenumber <= midpoint, np.cos(phase), np.sin(phase))
    boundary = (wavenumber == 0) | (wavenumber == midpoint)
    weights = np.where(boundary, math.sqrt(1.0 / length), math.sqrt(2.0 / length)).astype(np.float32)
    return (waveform * weights).astype(jnp.bfloat16)


def from_all(value):
    size = lax.axis_size("azi")
    blocks = [value]
    for shift in range(1, size):
        pairs = [(i, (i + shift) % size) for i in range(size)]
        blocks.append(lax.ppermute(value, "azi", pairs))
    return blocks


def from_twin(value):
    size = lax.axis_size("depth")
    return lax.ppermute(value, "depth", [(i, i ^ 1) for i in range(size)])


def body(table, heat_state, tangent_in, cotangent, wet_mask, sensors, propagators):
    slab, radial, local_azi = heat_state.shape
    size = lax.axis_size("azi")
    depth = lax.axis_size("depth")
    me = lax.axis_index("azi")
    core = lax.rem(lax.axis_index("depth"), 2)
    owners = [lax.rem(me - shift + size, size) for shift in range(size)]
    modes = propagators.shape[0]
    half = modes // 2

    mine = lax.dynamic_slice_in_dim(propagators, core * half, half, axis=0)
    other = from_twin(lax.dynamic_slice_in_dim(propagators, (1 - core) * half, half, axis=0))
    shard = jnp.concatenate(
        [jnp.where(core == 0, mine, other), jnp.where(core == 0, other, mine)], axis=1
    )
    groups = [list(range(c, depth, 2)) for c in range(2)]

    def gathered(block):
        return lax.all_gather(block, "depth", axis=1, tiled=True, axis_index_groups=groups)

    shards = from_all(shard)
    whole = [gathered(block) for block in shards]

    def rows(which):
        return [
            lax.dynamic_slice_in_dim(table, owner * modes + which * half, half, axis=0)
            for owner in owners
        ]

    def columns(weights):
        return [
            lax.dynamic_slice_in_dim(weights, owner * local_azi, local_azi, axis=1)
            for owner in owners
        ]

    own_rows, twin_rows = rows(core), rows(1 - core)
    to_modes = [columns(jnp.concatenate(r, axis=0)) for r in (own_rows, twin_rows)]
    to_azimuths = [
        [lax.dynamic_slice_in_dim(r, me * local_azi, local_azi, axis=1) for r in rs]
        for rs in (own_rows, twin_rows)
    ]

    def spectrum(blocks, which):
        total = 0.0
        for weights, block in zip(to_modes[which], blocks):
            total = total + jnp.einsum(
                "ka,zra->kzr", weights, block, preferred_element_type=jnp.float32
            )
        return total.astype(jnp.bfloat16)

    def transform(blocks):
        twin = from_twin(spectrum(blocks, 1))
        return jnp.concatenate([spectrum(blocks, 0), twin], axis=1)

    seed_blocks = from_all(cotangent.astype(jnp.bfloat16))
    forward_rhs, tangent_rhs = by_radius(
        rhs_kernel,
        wet_mask,
        [
            heat_state,
            *halo_planes(heat_state[-1:], heat_state[:1]),
            tangent_in,
            *halo_planes(tangent_in[-1:], tangent_in[:1]),
        ],
        [jnp.bfloat16] * 2,
    )
    forward_blocks = from_all(forward_rhs)
    tangent_blocks = from_all(tangent_rhs)

    def solve(spectra, formula):
        kept, received = [], []
        for c in range(size):
            solved = jnp.einsum(
                formula,
                whole[c],
                spectra[c * half : (c + 1) * half],
                preferred_element_type=jnp.float32,
            ).astype(jnp.bfloat16)
            kept.append(solved[:, :slab])
            received.append(from_twin(solved[:, slab:]))
        return kept, received

    def inverse(both):
        total = 0.0
        for weights, blocks in zip(to_azimuths, both):
            for w, block in zip(weights, blocks):
                total = total + jnp.einsum(
                    "ka,kzr->zra", w, block, preferred_element_type=jnp.float32
                )
        return total.astype(jnp.bfloat16)

    dual = inverse(solve(transform(seed_blocks), "ksr,kzs->kzr"))
    (gradient,) = by_radius(
        gradient_kernel, wet_mask, [heat_state, dual, *halo_planes(dual[-1:], dual[:1])], [jnp.float32]
    )

    new_state = inverse(solve(transform(forward_blocks), "krs,kzs->kzr"))
    radial_index = jnp.arange(radial, dtype=jnp.int32)[None, :, None]
    selected = jnp.where(radial_index == sensors[:, None, :], new_state, jnp.zeros_like(new_state))
    readings = jnp.sum(selected, axis=1)

    tangent_out = inverse(solve(transform(tangent_blocks), "krs,kzs->kzr"))
    return (new_state, tangent_out, gradient, readings)


def solution(mesh):
    def run(heat_state, tangent_in, cotangent, wet_mask, sensors, propagators):
        table = jnp.asarray(fourier_table(heat_state.shape[2]))
        field = P("depth", None, "azi")
        panel = P("depth", "azi")
        return jax.shard_map(
            body,
            mesh=mesh,
            in_specs=(P(), field, field, field, panel, panel, P("azi", "depth", None)),
            out_specs=(field, field, field, panel),
            check_vma=False,
        )(table, heat_state, tangent_in, cotangent, wet_mask, sensors, propagators)

    return run
```

```python
import functools
import math

import jax
import jax.numpy as jnp
import numpy as np
from jax import lax
from jax.experimental import pallas as pl
from jax.experimental.pallas import tpu as pltpu
from jax.sharding import PartitionSpec as P

mixing = 0.25
evaporation = 0.6
skin_depth = 16.0
mode_chunks = 2


def halo_planes(last, first):
    size = lax.axis_size("depth")
    up = [(i, i + 1) for i in range(size - 1)]
    down = [(j, i) for i, j in up]
    before = lax.ppermute(last, "depth", up)
    after = lax.ppermute(first, "depth", down)
    return before, after


def damping_profile(rows, lanes):
    radius = pl.program_id(0) * rows + lax.broadcasted_iota(jnp.int32, (rows, lanes), 0)
    return evaporation * jnp.exp(-radius.astype(jnp.float32) / skin_depth)


def plane(ref, before, after, z):
    source, index = (before, 0) if z < 0 else (after, 0) if z == ref.shape[0] else (ref, z)
    return source[index].astype(jnp.float32)


def mixed(ref, before, after, z):
    centre = plane(ref, before, after, z)
    around = plane(ref, before, after, z + 1) + plane(ref, before, after, z - 1)
    return centre, centre + mixing * (around - 2.0 * centre)


def rhs_kernel(wet, heat, heat_before, heat_after, tangent, tangent_before, tangent_after, out, tangent_out):
    slab, rows, lanes = heat.shape
    profile = damping_profile(rows, lanes)
    for z in range(slab):
        damping = wet[z : z + 1].astype(jnp.float32) * profile
        centre, value = mixed(heat, heat_before, heat_after, z)
        moisture = jnp.tanh(centre)
        out[z] = (value - damping * moisture).astype(out.dtype)
        slope = 1.0 - moisture * moisture
        centre, value = mixed(tangent, tangent_before, tangent_after, z)
        tangent_out[z] = (value - damping * slope * centre).astype(tangent_out.dtype)


def gradient_kernel(wet, heat, dual, dual_before, dual_after, out):
    slab, rows, lanes = heat.shape
    profile = damping_profile(rows, lanes)
    for z in range(slab):
        damping = wet[z : z + 1].astype(jnp.float32) * profile
        moisture = jnp.tanh(heat[z])
        slope = 1.0 - moisture * moisture
        centre, value = mixed(dual, dual_before, dual_after, z)
        out[z] = value - damping * slope * centre


def by_radius(kernel, wet, fields, dtypes):
    slab, radial, lanes = fields[0].shape
    rows = min(radial, 16)

    def spec(depth):
        return pl.BlockSpec((depth, rows, lanes), lambda i: (0, i, 0))

    count = len(dtypes) * slab * radial * lanes
    return pl.pallas_call(
        kernel,
        grid=(radial // rows,),
        in_specs=[pl.BlockSpec(wet.shape, lambda i: (0, 0))] + [spec(f.shape[0]) for f in fields],
        out_specs=[spec(slab) for _ in dtypes],
        out_shape=[jax.ShapeDtypeStruct((slab, radial, lanes), dtype) for dtype in dtypes],
        cost_estimate=pl.CostEstimate(flops=10 * count, bytes_accessed=6 * count, transcendentals=count),
    )(wet, *fields)


def fourier_table(length):
    wavenumber = np.arange(length, dtype=np.int32)[:, None]
    position = np.arange(length, dtype=np.int32)[None, :]
    midpoint = length // 2
    harmonic = np.where(wavenumber <= midpoint, wavenumber, wavenumber - midpoint)
    phase = (harmonic * position % length).astype(np.float32) * np.float32(2.0 * math.pi / length)
    waveform = np.where(wavenumber <= midpoint, np.cos(phase), np.sin(phase))
    boundary = (wavenumber == 0) | (wavenumber == midpoint)
    weights = np.where(boundary, math.sqrt(1.0 / length), math.sqrt(2.0 / length)).astype(np.float32)
    return (waveform * weights).astype(jnp.bfloat16)


def from_all(value):
    size = lax.axis_size("azi")
    blocks = [value]
    for shift in range(1, size):
        pairs = [(i, (i + shift) % size) for i in range(size)]
        blocks.append(lax.ppermute(value, "azi", pairs))
    return blocks


def split_body(table, heat_state, tangent_in, cotangent, wet_mask, sensors, propagators):
    slab, radial, local_azi = heat_state.shape
    size = lax.axis_size("azi")
    me = lax.axis_index("azi")
    owners = [lax.rem(me - shift + size, size) for shift in range(size)]
    modes = propagators.shape[0]
    step = modes // mode_chunks

    whole = [
        lax.all_gather(propagators[c * step : (c + 1) * step], "depth", axis=1, tiled=True)
        for c in range(mode_chunks)
    ]

    own_modes = lax.dynamic_slice_in_dim(table, me * modes, modes, axis=0)
    to_modes = [
        lax.dynamic_slice_in_dim(own_modes, owner * local_azi, local_azi, axis=1) for owner in owners
    ]
    own_azimuths = lax.dynamic_slice_in_dim(table, me * local_azi, local_azi, axis=1)
    to_azimuths = [
        lax.dynamic_slice_in_dim(own_azimuths, owner * modes, modes, axis=0) for owner in owners
    ]

    def part_spectrum(weights, block, c):
        return jnp.einsum(
            "ka,zra->kzr",
            weights[c * step : (c + 1) * step],
            block,
            preferred_element_type=jnp.float32,
        )

    seed_blocks = from_all(cotangent.astype(jnp.bfloat16))
    seed_part, heat_last, heat_first, tangent_last, tangent_first = lax.optimization_barrier(
        (
            part_spectrum(to_modes[0], seed_blocks[0], 0),
            heat_state[-1:],
            heat_state[:1],
            tangent_in[-1:],
            tangent_in[:1],
        )
    )

    forward_rhs, tangent_rhs = by_radius(
        rhs_kernel,
        wet_mask,
        [heat_state, *halo_planes(heat_last, heat_first), tangent_in, *halo_planes(tangent_last, tangent_first)],
        [jnp.bfloat16] * 2,
    )
    own_seed, forward_rhs, tangent_rhs = lax.optimization_barrier(
        (seed_blocks[0], forward_rhs, tangent_rhs)
    )
    seed_blocks = [own_seed] + seed_blocks[1:]
    forward_blocks = from_all(forward_rhs)
    tangent_blocks = from_all(tangent_rhs)

    def solve(blocks, formula, first=None):
        returned = []
        for c in range(mode_chunks):
            known = c == 0 and first is not None
            total = first if known else part_spectrum(to_modes[0], blocks[0], c)
            for weights, block in zip(to_modes[1:], blocks[1:]):
                total = total + part_spectrum(weights, block, c)
            solved = jnp.einsum(
                formula, whole[c], total.astype(jnp.bfloat16), preferred_element_type=jnp.float32
            ).astype(jnp.bfloat16)
            returned.append(from_all(solved))
        return returned

    def part_inverse(returned, pairs):
        total = 0.0
        for c, i in pairs:
            total = total + jnp.einsum(
                "ka,kzr->zra",
                to_azimuths[i][c * step : (c + 1) * step],
                returned[c][i],
                preferred_element_type=jnp.float32,
            )
        return total

    pairs = [(c, i) for i in range(size) for c in range(mode_chunks)]

    def inverse(returned):
        return part_inverse(returned, pairs).astype(jnp.bfloat16)

    dual_modes = solve(seed_blocks, "ksr,kzs->kzr", seed_part)
    dual_modes[0][0], *forward_received = lax.optimization_barrier(
        (dual_modes[0][0], *forward_blocks[1:])
    )
    forward_blocks = forward_blocks[:1] + forward_received
    forward_modes = solve(forward_blocks, "krs,kzs->kzr")
    tangent_modes = solve(tangent_blocks, "krs,kzs->kzr")

    dual = inverse(dual_modes)
    (gradient,) = by_radius(
        gradient_kernel, wet_mask, [heat_state, dual, *halo_planes(dual[-1:], dual[:1])], [jnp.float32]
    )

    new_state = inverse(forward_modes)
    radial_index = jnp.arange(radial, dtype=jnp.int32)[None, :, None]
    selected = jnp.where(radial_index == sensors[:, None, :], new_state, jnp.zeros_like(new_state))
    readings = jnp.sum(selected, axis=1)

    partial = part_inverse(tangent_modes, pairs[:-1])
    gradient, partial, tangent_modes[-1][-1] = lax.optimization_barrier(
        (gradient, partial, tangent_modes[-1][-1])
    )
    tangent_out = (partial + part_inverse(tangent_modes, pairs[-1:])).astype(jnp.bfloat16)
    return (new_state, tangent_out, gradient, readings)


fields = 3
blocks = 8
early = blocks // 2
own, other = 0, 1


def line_order():
    first = [(q, own, p) for p in range(3) for q in range(early)]
    later = [(q, own) for q in range(early, blocks)] + [(blocks - 1, other)]
    return first + [(q, c, p) for p in range(3) for q, c in later]


def pair_order():
    first = [(q, s) for s in range(4) for q in range(early)]
    first.insert(10, (blocks - 1, 0))
    return first + [(q, s) for s in range(4) for q in range(early, blocks - 1)]


def modes_kernel(
    shard, weights, seed, forward, tangent,
    out_seed, out_forward, out_tangent,
    matrices, table, values, stage, mine, theirs, given,
    pair_send, pair_recv, up_send, up_recv, down_send, down_recv, azi_send, azi_recv,
    twin_send, twin_recv, back_send, back_recv, keep_sem, load_sem,
):
    sources, outs = (seed, forward, tangent), (out_seed, out_forward, out_tangent)
    flips = (True, False, False)
    place, azi = lax.axis_index("depth"), lax.axis_index("azi")
    z, x, core = place // 4, place // 2 % 2, place % 2
    pair, twin, up, down = place + 2 - 4 * x, place + 1 - 2 * core, place + 4, place - 4
    count, radial, _ = matrices.shape
    step = count // blocks
    half = count // 2
    rows = shard.shape[1]
    slab = mine.shape[2]
    local = seed.shape[1]
    planes = slab // blocks
    mesh_ids = pl.DeviceIdType.MESH

    barrier = pltpu.get_barrier_semaphore()

    def greet(where, azimuth):
        pl.semaphore_signal(barrier, inc=1, device_id=(where, azimuth), device_id_type=mesh_ids)

    greet(pair, azi)
    greet(twin, azi)
    greet(place, 1 - azi)

    @pl.when(z < 3)
    def _():
        greet(up, azi)

    @pl.when(z > 0)
    def _():
        greet(down, azi)

    pl.semaphore_wait(barrier, 4 + (z + 1) // 2 % 2)

    def remote(src, dst, send, recv, where, azimuth=azi):
        return pltpu.make_async_remote_copy(
            src_ref=src, dst_ref=dst, send_sem=send, recv_sem=recv,
            device_id=(where, azimuth), device_id_type=mesh_ids,
        )

    def region(q, line, side):
        at = pl.multiple_of(rows * (2 * line + side), rows)
        return matrices.at[pl.ds(q * step, step), pl.ds(at, rows), :]

    flipped = (z, z + 1 - 2 * (z % 2), z + 2 - 4 * (z // 2), 3 - z)

    def pair_copy(q, s):
        ref = region(q, flipped[s], x)
        return remote(ref, ref, pair_send.at[q, s], pair_recv.at[q, s], pair)

    def line_item(q, c):
        return blocks if c == other else q

    def up_copy(q, c, p):
        ref = region(q, z - p, x if c == own else 1 - x)
        k = line_item(q, c)
        return remote(ref, ref, up_send.at[k, p], up_recv.at[k, p], up)

    def down_copy(q, c, p):
        ref = region(q, z + p, x if c == own else 1 - x)
        k = line_item(q, c)
        return remote(ref, ref, down_send.at[k, p], down_recv.at[k, p], down)

    def azi_copy(n):
        if n < early:
            return remote(
                region(n, z, x), region(n + early, z, x), azi_send.at[n], azi_recv.at[n], place, 1 - azi
            )
        f, part = divmod(n - early, blocks)
        span = planes * radial
        at = pl.ds(part * span, span)
        return remote(
            values.at[f, at, pl.ds(0, local)],
            values.at[f, at, pl.ds(local, local)],
            azi_send.at[n], azi_recv.at[n], place, 1 - azi,
        )

    pairs, lines, azis = pair_order(), line_order(), early + fields * blocks

    def send(t):
        if t < len(pairs):
            pair_copy(*pairs[t]).start()
        if t < azis:
            azi_copy(t).start()
        if t < len(lines):
            q, c, p = lines[t]

            @pl.when((z < 3) & (z >= p))
            def _():
                up_copy(q, c, p).start()

            @pl.when((z > 0) & (z + p <= 3))
            def _():
                down_copy(q, c, p).start()

    def receive(t):
        if 0 <= t < len(pairs):
            pair_copy(*pairs[t]).wait_recv()
        if 0 <= t < azis:
            azi_copy(t).wait_recv()
        if 0 <= t < len(lines):
            q, c, p = lines[t]

            @pl.when(z >= p + 1)
            def _():
                up_copy(q, c, p).wait_recv()

            @pl.when(z + p + 1 <= 3)
            def _():
                down_copy(q, c, p).wait_recv()

    def sent(t):
        if t < len(pairs):
            pair_copy(*pairs[t]).wait_send()
        if t < azis:
            azi_copy(t).wait_send()
        if t < len(lines):
            q, c, p = lines[t]

            @pl.when((z < 3) & (z >= p))
            def _():
                up_copy(q, c, p).wait_send()

            @pl.when((z > 0) & (z + p <= 3))
            def _():
                down_copy(q, c, p).wait_send()

    at = pl.multiple_of(rows * (2 * z + x), rows)
    loads = [pltpu.make_async_copy(shard, matrices.at[pl.ds(0, half), pl.ds(at, rows), :], load_sem.at[0])]
    for f in range(fields):
        loads.append(
            pltpu.make_async_copy(sources[f], values.at[f, :, pl.ds(0, local)], load_sem.at[1 + f])
        )
    loads.append(pltpu.make_async_copy(weights, table, load_sem.at[1 + fields]))
    for load in loads:
        load.start()
    for load in loads:
        load.wait()

    def twin_copy(f, part):
        at = pl.ds(part * half, half)
        return remote(
            given.at[f, at], theirs.at[f, at], twin_send.at[f, part], twin_recv.at[f, part], twin
        )

    def transform(f, part):
        into, first = (given, part) if part < 2 else (mine, part - 2)

        def planes_step(n, _):
            cols = values[f, pl.ds(pl.multiple_of(n * 2 * radial, 2 * radial), 2 * radial), :]
            out = lax.dot_general(
                table[pl.ds(part * half, half), :], cols, (((1,), (1,)), ((), ())),
                preferred_element_type=jnp.float32,
            )
            stage[pl.ds(pl.multiple_of(n * 2 * half, half), half), :] = out[:, :radial]
            stage[pl.ds(pl.multiple_of(n * 2 * half + half, half), half), :] = out[:, radial:]
            return 0

        lax.fori_loop(0, slab // 2, planes_step, 0)

        def turn(n, _):
            for u in range(8):
                k = n * 8 + u
                into[f, first * half + k] = stage[pl.ds(k, slab, stride=half), :].astype(jnp.bfloat16)
            return 0

        lax.fori_loop(0, half // 8, turn, 0)
        if part < 2:
            twin_copy(f, part).start()

    def keep_copy(f, q):
        at = pl.ds(q * step, step)
        return pltpu.make_async_copy(mine.at[f, at], outs[f].at[at], keep_sem.at[f, q])

    def back_copy(f, q):
        return remote(
            theirs.at[f, pl.ds(q * step, step)],
            outs[f].at[pl.ds(count + q * step, step)],
            back_send.at[f, q], back_recv.at[f, q], twin,
        )

    def solve(which, q):
        def one(n, _):
            for u in range(4):
                k = q * step + n * 4 + u
                matrix = matrices[k]
                for flip in (True, False):
                    chosen = [f for f in which if flips[f] == flip]
                    if not chosen:
                        continue
                    stacked = jnp.concatenate(
                        [part[f, k] for f in chosen for part in (mine, theirs)], axis=0
                    )
                    out = lax.dot_general(
                        stacked, matrix, (((1,), (0 if flip else 1,)), ((), ())),
                        preferred_element_type=jnp.float32,
                    ).astype(jnp.bfloat16)
                    for i, f in enumerate(chosen):
                        mine[f, k] = out[2 * i * slab : (2 * i + 1) * slab]
                        theirs[f, k] = out[(2 * i + 1) * slab : (2 * i + 2) * slab]
            return 0

        lax.fori_loop(0, step // 4, one, 0)
        for f in which:
            keep_copy(f, q).start()
            back_copy(f, q).start()

    def met(f):
        for part in range(2):
            twin_copy(f, part).wait_recv()

    tasks = {
        13: [lambda: transform(0, 0), lambda: transform(0, 1)],
        14: [lambda: transform(0, 2), lambda: transform(0, 3)],
        16: [lambda: met(0), lambda: solve([0], 0)],
        17: [lambda: solve([0], 1), lambda: solve([0], 2)],
        18: [lambda: solve([0], 3)],
        21: [lambda: transform(1, 0), lambda: transform(1, 1)],
        22: [lambda: transform(1, 2), lambda: transform(1, 3)],
        24: [lambda: met(1), lambda: solve([1], 0), lambda: solve([1], 1)],
        25: [lambda: solve([1], 2)],
        26: [lambda: solve([1], 3)],
        29: [functools.partial(transform, 2, part) for part in range(4)]
        + [lambda: solve([0, 1], 4)],
        30: [lambda: solve([0, 1], 7), lambda: solve([0, 1], 5), lambda: met(2)]
        + [functools.partial(solve, [2], q) for q in (0, 1, 2, 3, 4, 7, 5)],
        31: [lambda: solve([0, 1, 2], 6)],
    }

    lag = 2
    for t in range(32):
        receive(t - lag)
        send(t)
        for task in tasks.get(t, []):
            task()

    for t in range(32):
        sent(t)
    for f in range(fields):
        for part in range(2):
            twin_copy(f, part).wait_send()
        for q in range(blocks):
            keep_copy(f, q).wait()
            back_copy(f, q).wait()


def solved_modes(shard, weights, seed, forward, tangent):
    slab, radial, local = seed.shape
    half, rows, _ = shard.shape
    count = 2 * half
    dma = pltpu.SemaphoreType.DMA
    flat = [v.reshape(slab * radial, local) for v in (seed, forward, tangent)]
    out = jax.ShapeDtypeStruct((2 * count, slab, radial), jnp.bfloat16)
    return pl.pallas_call(
        modes_kernel,
        out_shape=[out] * fields,
        in_specs=[pl.BlockSpec(memory_space=pl.ANY)] * 5,
        out_specs=[pl.BlockSpec(memory_space=pl.ANY)] * fields,
        scratch_shapes=[
            pltpu.VMEM((count, radial, radial), jnp.bfloat16),
            pltpu.VMEM((2 * count, 2 * local), jnp.bfloat16),
            pltpu.VMEM((fields, slab * radial, 2 * local), jnp.bfloat16),
            pltpu.VMEM((slab * half, radial), jnp.float32),
            pltpu.VMEM((fields, count, slab, radial), jnp.bfloat16),
            pltpu.VMEM((fields, count, slab, radial), jnp.bfloat16),
            pltpu.VMEM((fields, count, slab, radial), jnp.bfloat16),
            dma((blocks, 4)), dma((blocks, 4)),
            dma((blocks + 1, 3)), dma((blocks + 1, 3)),
            dma((blocks + 1, 3)), dma((blocks + 1, 3)),
            dma((early + fields * blocks,)), dma((early + fields * blocks,)),
            dma((fields, 2)), dma((fields, 2)),
            dma((fields, blocks)), dma((fields, blocks)), dma((fields, blocks)),
            dma((fields + 2,)),
        ],
        compiler_params=pltpu.CompilerParams(
            collective_id=0, has_side_effects=True, vmem_limit_bytes=58 * 1024 * 1024
        ),
        cost_estimate=pl.CostEstimate(flops=15 * 10**9, bytes_accessed=10**8, transcendentals=0),
    )(shard, weights, *flat)


def fused_body(table, heat_state, tangent_in, cotangent, wet_mask, sensors, propagators):
    slab, radial, local_azi = heat_state.shape
    depth = lax.axis_size("depth")
    me = lax.axis_index("azi")
    core = lax.rem(lax.axis_index("depth"), 2)
    modes = propagators.shape[0]
    half = modes // 2

    mine = lax.dynamic_slice_in_dim(propagators, core * half, half, axis=0)
    outgoing = lax.dynamic_slice_in_dim(propagators, (1 - core) * half, half, axis=0)
    incoming = lax.ppermute(outgoing, "depth", [(i, i ^ 1) for i in range(depth)])
    shard = jnp.concatenate(
        [jnp.where(core == 0, mine, incoming), jnp.where(core == 0, incoming, mine)], axis=1
    )

    def table_rows(which):
        return [
            lax.dynamic_slice_in_dim(table, owner * modes + which * half, half, axis=0)
            for owner in (me, 1 - me)
        ]

    own_rows = jnp.concatenate(table_rows(core), axis=0)
    twin_rows = jnp.concatenate(table_rows(1 - core), axis=0)

    def columns(weights, owner):
        return lax.dynamic_slice_in_dim(weights, owner * local_azi, local_azi, axis=1)

    weights = jnp.concatenate([twin_rows, own_rows], axis=0)
    weights = jnp.concatenate([columns(weights, me), columns(weights, 1 - me)], axis=1)
    to_azimuths = columns(jnp.concatenate([own_rows, twin_rows], axis=0), me)

    forward_rhs, tangent_rhs = by_radius(
        rhs_kernel,
        wet_mask,
        [
            heat_state,
            *halo_planes(heat_state[-1:], heat_state[:1]),
            tangent_in,
            *halo_planes(tangent_in[-1:], tangent_in[:1]),
        ],
        [jnp.bfloat16] * 2,
    )
    dual_modes, forward_modes, tangent_modes = solved_modes(
        shard, weights, cotangent.astype(jnp.bfloat16), forward_rhs, tangent_rhs
    )

    def inverse(solved):
        return jnp.einsum(
            "ka,kzr->zra", to_azimuths, solved, preferred_element_type=jnp.float32
        ).astype(jnp.bfloat16)

    dual = inverse(dual_modes)
    (gradient,) = by_radius(
        gradient_kernel, wet_mask, [heat_state, dual, *halo_planes(dual[-1:], dual[:1])], [jnp.float32]
    )
    new_state = inverse(forward_modes)
    radial_index = jnp.arange(radial, dtype=jnp.int32)[None, :, None]
    selected = jnp.where(radial_index == sensors[:, None, :], new_state, jnp.zeros_like(new_state))
    readings = jnp.sum(selected, axis=1)
    tangent_out = inverse(tangent_modes)
    return (new_state, tangent_out, gradient, readings)


def solution(mesh):
    def run(heat_state, tangent_in, cotangent, wet_mask, sensors, propagators):
        table = jnp.asarray(fourier_table(heat_state.shape[2]))
        field = P("depth", None, "azi")
        fits = mesh.shape["azi"] == 2 and mesh.shape["depth"] == 16
        body = fused_body if fits else split_body
        panel = P("depth", "azi")
        return jax.shard_map(
            body,
            mesh=mesh,
            in_specs=(P(), field, field, field, panel, panel, P("azi", "depth", None)),
            out_specs=(field, field, field, panel),
            check_vma=False,
        )(table, heat_state, tangent_in, cotangent, wet_mask, sensors, propagators)

    return run
```

```python
import functools
import math

import jax
import jax.numpy as jnp
import numpy as np
from jax import lax
from jax.experimental import pallas as pl
from jax.experimental.pallas import tpu as pltpu
from jax.sharding import PartitionSpec as P

mixing = 0.25
evaporation = 0.6
skin_depth = 16.0
mode_chunks = 2


def halo_planes(last, first):
    size = lax.axis_size("depth")
    up = [(i, i + 1) for i in range(size - 1)]
    down = [(j, i) for i, j in up]
    before = lax.ppermute(last, "depth", up)
    after = lax.ppermute(first, "depth", down)
    return before, after


def damping_profile(rows, lanes):
    radius = pl.program_id(0) * rows + lax.broadcasted_iota(jnp.int32, (rows, lanes), 0)
    return evaporation * jnp.exp(-radius.astype(jnp.float32) / skin_depth)


def plane(ref, before, after, z):
    source, index = (before, 0) if z < 0 else (after, 0) if z == ref.shape[0] else (ref, z)
    return source[index].astype(jnp.float32)


def mixed(ref, before, after, z):
    centre = plane(ref, before, after, z)
    around = plane(ref, before, after, z + 1) + plane(ref, before, after, z - 1)
    return centre, centre + mixing * (around - 2.0 * centre)


def rhs_kernel(wet, heat, heat_before, heat_after, tangent, tangent_before, tangent_after, out, tangent_out):
    slab, rows, lanes = heat.shape
    profile = damping_profile(rows, lanes)
    for z in range(slab):
        damping = wet[z : z + 1].astype(jnp.float32) * profile
        centre, value = mixed(heat, heat_before, heat_after, z)
        moisture = jnp.tanh(centre)
        out[z] = (value - damping * moisture).astype(out.dtype)
        slope = 1.0 - moisture * moisture
        centre, value = mixed(tangent, tangent_before, tangent_after, z)
        tangent_out[z] = (value - damping * slope * centre).astype(tangent_out.dtype)


def gradient_kernel(wet, heat, dual, dual_before, dual_after, out):
    slab, rows, lanes = heat.shape
    profile = damping_profile(rows, lanes)
    for z in range(slab):
        damping = wet[z : z + 1].astype(jnp.float32) * profile
        moisture = jnp.tanh(heat[z])
        slope = 1.0 - moisture * moisture
        centre, value = mixed(dual, dual_before, dual_after, z)
        out[z] = value - damping * slope * centre


def by_radius(kernel, wet, fields, dtypes):
    slab, radial, lanes = fields[0].shape
    rows = min(radial, 16)

    def spec(depth):
        return pl.BlockSpec((depth, rows, lanes), lambda i: (0, i, 0))

    count = len(dtypes) * slab * radial * lanes
    return pl.pallas_call(
        kernel,
        grid=(radial // rows,),
        in_specs=[pl.BlockSpec(wet.shape, lambda i: (0, 0))] + [spec(f.shape[0]) for f in fields],
        out_specs=[spec(slab) for _ in dtypes],
        out_shape=[jax.ShapeDtypeStruct((slab, radial, lanes), dtype) for dtype in dtypes],
        cost_estimate=pl.CostEstimate(flops=10 * count, bytes_accessed=6 * count, transcendentals=count),
    )(wet, *fields)


def fourier_table(length):
    wavenumber = np.arange(length, dtype=np.int32)[:, None]
    position = np.arange(length, dtype=np.int32)[None, :]
    midpoint = length // 2
    harmonic = np.where(wavenumber <= midpoint, wavenumber, wavenumber - midpoint)
    phase = (harmonic * position % length).astype(np.float32) * np.float32(2.0 * math.pi / length)
    waveform = np.where(wavenumber <= midpoint, np.cos(phase), np.sin(phase))
    boundary = (wavenumber == 0) | (wavenumber == midpoint)
    weights = np.where(boundary, math.sqrt(1.0 / length), math.sqrt(2.0 / length)).astype(np.float32)
    return (waveform * weights).astype(jnp.bfloat16)


def from_all(value):
    size = lax.axis_size("azi")
    blocks = [value]
    for shift in range(1, size):
        pairs = [(i, (i + shift) % size) for i in range(size)]
        blocks.append(lax.ppermute(value, "azi", pairs))
    return blocks


def split_body(table, heat_state, tangent_in, cotangent, wet_mask, sensors, propagators):
    slab, radial, local_azi = heat_state.shape
    size = lax.axis_size("azi")
    me = lax.axis_index("azi")
    owners = [lax.rem(me - shift + size, size) for shift in range(size)]
    modes = propagators.shape[0]
    step = modes // mode_chunks

    whole = [
        lax.all_gather(propagators[c * step : (c + 1) * step], "depth", axis=1, tiled=True)
        for c in range(mode_chunks)
    ]

    own_modes = lax.dynamic_slice_in_dim(table, me * modes, modes, axis=0)
    to_modes = [
        lax.dynamic_slice_in_dim(own_modes, owner * local_azi, local_azi, axis=1) for owner in owners
    ]
    own_azimuths = lax.dynamic_slice_in_dim(table, me * local_azi, local_azi, axis=1)
    to_azimuths = [
        lax.dynamic_slice_in_dim(own_azimuths, owner * modes, modes, axis=0) for owner in owners
    ]

    def part_spectrum(weights, block, c):
        return jnp.einsum(
            "ka,zra->kzr",
            weights[c * step : (c + 1) * step],
            block,
            preferred_element_type=jnp.float32,
        )

    seed_blocks = from_all(cotangent.astype(jnp.bfloat16))
    seed_part, heat_last, heat_first, tangent_last, tangent_first = lax.optimization_barrier(
        (
            part_spectrum(to_modes[0], seed_blocks[0], 0),
            heat_state[-1:],
            heat_state[:1],
            tangent_in[-1:],
            tangent_in[:1],
        )
    )

    forward_rhs, tangent_rhs = by_radius(
        rhs_kernel,
        wet_mask,
        [heat_state, *halo_planes(heat_last, heat_first), tangent_in, *halo_planes(tangent_last, tangent_first)],
        [jnp.bfloat16] * 2,
    )
    own_seed, forward_rhs, tangent_rhs = lax.optimization_barrier(
        (seed_blocks[0], forward_rhs, tangent_rhs)
    )
    seed_blocks = [own_seed] + seed_blocks[1:]
    forward_blocks = from_all(forward_rhs)
    tangent_blocks = from_all(tangent_rhs)

    def solve(blocks, formula, first=None):
        returned = []
        for c in range(mode_chunks):
            known = c == 0 and first is not None
            total = first if known else part_spectrum(to_modes[0], blocks[0], c)
            for weights, block in zip(to_modes[1:], blocks[1:]):
                total = total + part_spectrum(weights, block, c)
            solved = jnp.einsum(
                formula, whole[c], total.astype(jnp.bfloat16), preferred_element_type=jnp.float32
            ).astype(jnp.bfloat16)
            returned.append(from_all(solved))
        return returned

    def part_inverse(returned, pairs):
        total = 0.0
        for c, i in pairs:
            total = total + jnp.einsum(
                "ka,kzr->zra",
                to_azimuths[i][c * step : (c + 1) * step],
                returned[c][i],
                preferred_element_type=jnp.float32,
            )
        return total

    pairs = [(c, i) for i in range(size) for c in range(mode_chunks)]

    def inverse(returned):
        return part_inverse(returned, pairs).astype(jnp.bfloat16)

    dual_modes = solve(seed_blocks, "ksr,kzs->kzr", seed_part)
    dual_modes[0][0], *forward_received = lax.optimization_barrier(
        (dual_modes[0][0], *forward_blocks[1:])
    )
    forward_blocks = forward_blocks[:1] + forward_received
    forward_modes = solve(forward_blocks, "krs,kzs->kzr")
    tangent_modes = solve(tangent_blocks, "krs,kzs->kzr")

    dual = inverse(dual_modes)
    (gradient,) = by_radius(
        gradient_kernel, wet_mask, [heat_state, dual, *halo_planes(dual[-1:], dual[:1])], [jnp.float32]
    )

    new_state = inverse(forward_modes)
    radial_index = jnp.arange(radial, dtype=jnp.int32)[None, :, None]
    selected = jnp.where(radial_index == sensors[:, None, :], new_state, jnp.zeros_like(new_state))
    readings = jnp.sum(selected, axis=1)

    partial = part_inverse(tangent_modes, pairs[:-1])
    gradient, partial, tangent_modes[-1][-1] = lax.optimization_barrier(
        (gradient, partial, tangent_modes[-1][-1])
    )
    tangent_out = (partial + part_inverse(tangent_modes, pairs[-1:])).astype(jnp.bfloat16)
    return (new_state, tangent_out, gradient, readings)


fields = 3
blocks = 8
early = blocks // 2
own, other = 0, 1


def line_order():
    first = [(q, own, p) for p in range(3) for q in range(early)]
    later = [(q, own) for q in range(early, blocks)] + [(blocks - 1, other)]
    return first + [(q, c, p) for p in range(3) for q, c in later]


def pair_order():
    first = [(q, s) for s in range(4) for q in range(early)]
    first.insert(10, (blocks - 1, 0))
    return first + [(q, s) for s in range(4) for q in range(early, blocks - 1)]


def modes_kernel(
    shard, full, cotangent, heat, tangent, wet,
    out_seed, out_forward, out_tangent,
    matrices, table, values, stage, mine, theirs, given, raw, edges, damp,
    pair_send, pair_recv, up_send, up_recv, down_send, down_recv, azi_send, azi_recv,
    twin_send, twin_recv, back_send, back_recv, keep_sem, load_sem, table_sem, raw_sem, edge_send, edge_recv,
):
    outs = (out_seed, out_forward, out_tangent)
    flips = (True, False, False)
    place, azi = lax.axis_index("depth"), lax.axis_index("azi")
    z, x, core = place // 4, place // 2 % 2, place % 2
    pair, twin, up, down = place + 2 - 4 * x, place + 1 - 2 * core, place + 4, place - 4
    count, radial, _ = matrices.shape
    step = count // blocks
    half = count // 2
    rows = shard.shape[1]
    slab = mine.shape[2]
    local = heat.shape[2]
    strip = raw.shape[3]
    strips = radial // strip
    last = lax.axis_size("depth") - 1
    planes = slab // blocks
    mesh_ids = pl.DeviceIdType.MESH

    barrier = pltpu.get_barrier_semaphore()

    def greet(where, azimuth):
        pl.semaphore_signal(barrier, inc=1, device_id=(where, azimuth), device_id_type=mesh_ids)

    greet(pair, azi)
    greet(twin, azi)
    greet(place, 1 - azi)

    @pl.when(z < 3)
    def _():
        greet(up, azi)

    @pl.when(z > 0)
    def _():
        greet(down, azi)

    @pl.when(place < last)
    def _():
        greet(place + 1, azi)

    @pl.when(place > 0)
    def _():
        greet(place - 1, azi)

    inner = (place + last) // (last + 1) + (2 * last - place) // (last + 1)
    pl.semaphore_wait(barrier, 4 + (z + 1) // 2 % 2 + inner)

    def remote(src, dst, send, recv, where, azimuth=azi):
        return pltpu.make_async_remote_copy(
            src_ref=src, dst_ref=dst, send_sem=send, recv_sem=recv,
            device_id=(where, azimuth), device_id_type=mesh_ids,
        )

    def region(q, line, side):
        at = pl.multiple_of(rows * (2 * line + side), rows)
        return matrices.at[pl.ds(q * step, step), pl.ds(at, rows), :]

    flipped = (z, z + 1 - 2 * (z % 2), z + 2 - 4 * (z // 2), 3 - z)

    def pair_copy(q, s):
        ref = region(q, flipped[s], x)
        return remote(ref, ref, pair_send.at[q, s], pair_recv.at[q, s], pair)

    def line_item(q, c):
        return blocks if c == other else q

    def up_copy(q, c, p):
        ref = region(q, z - p, x if c == own else 1 - x)
        k = line_item(q, c)
        return remote(ref, ref, up_send.at[k, p], up_recv.at[k, p], up)

    def down_copy(q, c, p):
        ref = region(q, z + p, x if c == own else 1 - x)
        k = line_item(q, c)
        return remote(ref, ref, down_send.at[k, p], down_recv.at[k, p], down)

    def azi_copy(n):
        if n < early:
            return remote(
                region(n, z, x), region(n + early, z, x), azi_send.at[n], azi_recv.at[n], place, 1 - azi
            )
        f, part = divmod(n - early, blocks)
        span = planes * radial
        at = pl.ds(part * span, span)
        return remote(
            values.at[f, at, pl.ds(0, local)],
            values.at[f, at, pl.ds(local, local)],
            azi_send.at[n], azi_recv.at[n], place, 1 - azi,
        )

    pairs, lines, azis = pair_order(), line_order(), early + fields * blocks

    def send(t):
        if t < len(pairs):
            pair_copy(*pairs[t]).start()
        if t < azis:
            azi_copy(t).start()
        if t < len(lines):
            q, c, p = lines[t]

            @pl.when((z < 3) & (z >= p))
            def _():
                up_copy(q, c, p).start()

            @pl.when((z > 0) & (z + p <= 3))
            def _():
                down_copy(q, c, p).start()

    def receive(t):
        if 0 <= t < len(pairs):
            pair_copy(*pairs[t]).wait_recv()
        if 0 <= t < azis:
            azi_copy(t).wait_recv()
        if 0 <= t < len(lines):
            q, c, p = lines[t]

            @pl.when(z >= p + 1)
            def _():
                up_copy(q, c, p).wait_recv()

            @pl.when(z + p + 1 <= 3)
            def _():
                down_copy(q, c, p).wait_recv()

    def sent(t):
        if t < len(pairs):
            pair_copy(*pairs[t]).wait_send()
        if t < azis:
            azi_copy(t).wait_send()
        if t < len(lines):
            q, c, p = lines[t]

            @pl.when((z < 3) & (z >= p))
            def _():
                up_copy(q, c, p).wait_send()

            @pl.when((z > 0) & (z + p <= 3))
            def _():
                down_copy(q, c, p).wait_send()

    at = pl.multiple_of(rows * (2 * z + x), rows)
    shard_load = pltpu.make_async_copy(
        shard, matrices.at[pl.ds(0, half), pl.ds(at, rows), :], load_sem.at[0]
    )
    shard_load.start()
    damp_load = pltpu.make_async_copy(wet, damp, load_sem.at[1])
    damp_load.start()

    def strip_loads(n):
        slot = n % 2
        c = n % strips
        span = pl.ds(c * strip, strip)
        if n < strips:
            return [
                pltpu.make_async_copy(
                    cotangent.at[:, span, :], raw.at[slot, 0, pl.ds(1, slab)], raw_sem.at[slot, 0]
                )
            ]
        found = []
        for f, source in enumerate((heat, tangent)):
            found.append((source.at[:, span, :], raw.at[slot, f, pl.ds(1, slab)], 3 * f))
            found.append((edges.at[f, 0, span], raw.at[slot, f, 0], 3 * f + 1))
            found.append((edges.at[f, 1, span], raw.at[slot, f, slab + 1], 3 * f + 2))
        return [pltpu.make_async_copy(a, b, raw_sem.at[slot, i]) for a, b, i in found]

    for load in strip_loads(0):
        load.start()

    def edge_copies(side):
        out = []
        for f, source in enumerate((heat, tangent)):
            out.append(
                remote(
                    source.at[slab - 1 if side == 0 else 0], edges.at[f, side],
                    edge_send.at[f, side], edge_recv.at[f, side],
                    place + 1 if side == 0 else place - 1,
                )
            )
        return out

    def edges_out():
        @pl.when(place < last)
        def _():
            for copy in edge_copies(0):
                copy.start()

        @pl.when(place > 0)
        def _():
            for copy in edge_copies(1):
                copy.start()

    def edges_in():
        for side, empty, full_side in ((0, place == 0, place > 0), (1, place == last, place < last)):

            @pl.when(full_side)
            def _():
                for copy in edge_copies(side):
                    copy.wait_recv()

            @pl.when(empty)
            def _():
                edges[:, side] = jnp.zeros((2, radial, local), jnp.float32)

    def edges_sent():
        @pl.when(place < last)
        def _():
            for copy in edge_copies(0):
                copy.wait_send()

        @pl.when(place > 0)
        def _():
            for copy in edge_copies(1):
                copy.wait_send()

    table_loads = []
    for part in range(4):
        owner, which = (azi, 1 - azi)[part % 2], (1 - core, core)[part // 2]
        row = pl.multiple_of((2 * owner + which) * (half), half)
        for h in range(2):
            col = pl.multiple_of((azi, 1 - azi)[h] * local, local)
            table_loads.append(
                pltpu.make_async_copy(
                    full.at[pl.ds(row, half), pl.ds(col, local)],
                    table.at[pl.ds(part * half, half), pl.ds(h * local, local)],
                    table_sem.at[part, h],
                )
            )

    def prepare(n):
        slot = n % 2
        c = n % strips
        if n + 1 == strips:
            edges_in()
        if n + 1 < 2 * strips:
            for load in strip_loads(n + 1):
                load.start()
        for load in strip_loads(n):
            load.wait()
        radius = c * strip + lax.broadcasted_iota(jnp.int32, (strip, local), 0)
        profile = evaporation * jnp.exp(-radius.astype(jnp.float32) / skin_depth)

        def plane_step(p, _):
            into = pl.ds(pl.multiple_of(p * radial + c * strip, strip), strip)
            if n < strips:
                values[0, into, pl.ds(0, local)] = raw[slot, 0, p + 1].astype(jnp.bfloat16)
                return 0
            damping = damp[pl.ds(p, 1), :].astype(jnp.float32) * profile

            def mix(f):
                centre = raw[slot, f, p + 1]
                around = raw[slot, f, p + 2] + raw[slot, f, p]
                return centre, centre + mixing * (around - 2.0 * centre)

            centre, value = mix(0)
            moisture = jnp.tanh(centre)
            values[1, into, pl.ds(0, local)] = (value - damping * moisture).astype(jnp.bfloat16)
            slope = 1.0 - moisture * moisture
            centre, value = mix(1)
            values[2, into, pl.ds(0, local)] = (value - damping * slope * centre).astype(jnp.bfloat16)
            return 0

        lax.fori_loop(0, slab, plane_step, 0)

    def twin_copy(f, part):
        at = pl.ds(part * half, half)
        return remote(
            given.at[f, at], theirs.at[f, at], twin_send.at[f, part], twin_recv.at[f, part], twin
        )

    group = 4

    def transform(f, into, first):
        def planes_step(n, _):
            span = group * radial
            cols = values[f, pl.ds(pl.multiple_of(n * span, span), span), :]
            out = lax.dot_general(
                table[pl.ds(first, count), :], cols, (((1,), (1,)), ((), ())),
                preferred_element_type=jnp.float32,
            )
            for g in range(group):
                at = pl.multiple_of((n * group + g) * count, count)
                stage[pl.ds(at, count), :] = out[:, g * radial : (g + 1) * radial]
            return 0

        lax.fori_loop(0, slab // group, planes_step, 0)

        def turn(n, _):
            for u in range(8):
                k = n * 8 + u
                into[f, k] = stage[pl.ds(k, slab, stride=count), :].astype(jnp.bfloat16)
            return 0

        for part in range(2):
            lax.fori_loop(part * half // 8, (part + 1) * half // 8, turn, 0)
            if first == 0:
                twin_copy(f, part).start()

    def give(f):
        transform(f, given, 0)

    def take(f):
        transform(f, mine, count)

    def keep_copy(f, q):
        at = pl.ds(q * step, step)
        return pltpu.make_async_copy(mine.at[f, at], outs[f].at[at], keep_sem.at[f, q])

    def back_copy(f, q):
        return remote(
            theirs.at[f, pl.ds(q * step, step)],
            outs[f].at[pl.ds(count + q * step, step)],
            back_send.at[f, q], back_recv.at[f, q], twin,
        )

    def solve(which, q):
        def one(n, _):
            found = []
            for u in range(16):
                k = q * step + n * 16 + u
                matrix = matrices[k]
                for flip in (True, False):
                    chosen = [f for f in which if flips[f] == flip]
                    if not chosen:
                        continue
                    stacked = jnp.concatenate(
                        [part[f, k] for f in chosen for part in (mine, theirs)], axis=0
                    )
                    out = lax.dot_general(
                        stacked, matrix, (((1,), (0 if flip else 1,)), ((), ())),
                        preferred_element_type=jnp.float32,
                    )
                    found.append((chosen, k, out))
            for chosen, k, out in found:
                out = out.astype(jnp.bfloat16)
                for i, f in enumerate(chosen):
                    mine[f, k] = out[2 * i * slab : (2 * i + 1) * slab]
                    theirs[f, k] = out[(2 * i + 1) * slab : (2 * i + 2) * slab]
            return 0

        lax.fori_loop(0, step // 16, one, 0)
        for f in which:
            keep_copy(f, q).start()
            back_copy(f, q).start()

    def met(f):
        for part in range(2):
            twin_copy(f, part).wait_recv()

    def begin():
        edges_out()
        for load in table_loads:
            load.start()
        damp_load.wait()
        for n in range(4):
            prepare(n)

    def table_in():
        for load in table_loads:
            load.wait()

    P = functools.partial
    tasks = {0: [begin], 1: [P(prepare, n) for n in range(4, strips)], 2: [table_in]}
    for n in range(strips):
        tasks.setdefault(2 + n, []).append(P(prepare, strips + n))
    tasks |= {
        13: [P(give, 0)],
        14: [P(take, 0)],
        16: [P(met, 0), P(solve, [0], 0), P(solve, [0], 1)],
        17: [P(solve, [0], 2)],
        18: [P(solve, [0], 3)],
        21: [P(give, 1)],
        22: [P(take, 1)],
        24: [P(met, 1), P(solve, [1], 0), P(solve, [1], 1)],
        25: [P(solve, [1], 2), P(solve, [1], 3)],
        28: [P(solve, [0], 4), P(solve, [0], 7)],
        29: [P(give, 2), P(take, 2), P(solve, [0], 5)],
        30: [P(solve, [0], 6), P(met, 2)]
        + [P(solve, [2], q) for q in range(early)]
        + [P(solve, [1, 2], q) for q in (4, 7, 5, 6)],
    }

    shard_load.wait()
    lag = 2
    for t in range(31):
        receive(t - lag)
        send(t)
        for task in tasks.get(t, []):
            task()

    edges_sent()
    for t in range(31):
        sent(t)
    for f in range(fields):
        for part in range(2):
            twin_copy(f, part).wait_send()
        for q in range(blocks):
            keep_copy(f, q).wait()
            back_copy(f, q).wait()


def solved_modes(shard, table, cotangent, heat, tangent, wet):
    slab, radial, local = heat.shape
    half, rows, _ = shard.shape
    count = 2 * half
    strip = 16
    dma = pltpu.SemaphoreType.DMA
    out = jax.ShapeDtypeStruct((2 * count, slab, radial), jnp.bfloat16)
    modes = pltpu.VMEM((fields, count, slab, radial), jnp.bfloat16)
    return pl.pallas_call(
        modes_kernel,
        out_shape=[out] * fields,
        in_specs=[pl.BlockSpec(memory_space=pl.ANY)] * 6,
        out_specs=[pl.BlockSpec(memory_space=pl.ANY)] * fields,
        scratch_shapes=[
            pltpu.VMEM((count, radial, radial), jnp.bfloat16),
            pltpu.VMEM((2 * count, 2 * local), jnp.bfloat16),
            pltpu.VMEM((fields, slab * radial, 2 * local), jnp.bfloat16),
            pltpu.VMEM((slab * count, radial), jnp.float32),
            modes,
            modes,
            modes,
            pltpu.VMEM((2, 2, slab + 2, strip, local), jnp.float32),
            pltpu.VMEM((2, 2, radial, local), jnp.float32),
            pltpu.VMEM((slab, local), jnp.int32),
            dma((blocks, 4)), dma((blocks, 4)),
            dma((blocks + 1, 3)), dma((blocks + 1, 3)),
            dma((blocks + 1, 3)), dma((blocks + 1, 3)),
            dma((early + fields * blocks,)), dma((early + fields * blocks,)),
            dma((fields, 2)), dma((fields, 2)),
            dma((fields, blocks)), dma((fields, blocks)), dma((fields, blocks)),
            dma((2,)), dma((4, 2)), dma((2, 6)), dma((2, 2)), dma((2, 2)),
        ],
        compiler_params=pltpu.CompilerParams(
            collective_id=0, has_side_effects=True, vmem_limit_bytes=60 * 1024 * 1024
        ),
        cost_estimate=pl.CostEstimate(flops=15 * 10**9, bytes_accessed=10**8, transcendentals=0),
    )(shard, table, cotangent, heat, tangent, wet)


def fused_body(table, heat_state, tangent_in, cotangent, wet_mask, sensors, propagators):
    slab, radial, local_azi = heat_state.shape
    depth = lax.axis_size("depth")
    me = lax.axis_index("azi")
    core = lax.rem(lax.axis_index("depth"), 2)
    modes = propagators.shape[0]
    half = modes // 2

    mine = lax.dynamic_slice_in_dim(propagators, core * half, half, axis=0)
    outgoing = lax.dynamic_slice_in_dim(propagators, (1 - core) * half, half, axis=0)
    incoming = lax.ppermute(outgoing, "depth", [(i, i ^ 1) for i in range(depth)])
    shard = jnp.concatenate(
        [jnp.where(core == 0, mine, incoming), jnp.where(core == 0, incoming, mine)], axis=1
    )

    def table_rows(which):
        return [
            lax.dynamic_slice_in_dim(table, owner * modes + which * half, half, axis=0)
            for owner in (me, 1 - me)
        ]

    own_rows = jnp.concatenate(table_rows(core), axis=0)
    twin_rows = jnp.concatenate(table_rows(1 - core), axis=0)

    def columns(weights, owner):
        return lax.dynamic_slice_in_dim(weights, owner * local_azi, local_azi, axis=1)

    to_azimuths = columns(jnp.concatenate([own_rows, twin_rows], axis=0), me)

    dual_modes, forward_modes, tangent_modes = solved_modes(
        shard, table, cotangent, heat_state, tangent_in, wet_mask
    )

    def inverse(solved):
        return jnp.einsum(
            "ka,kzr->zra", to_azimuths, solved, preferred_element_type=jnp.float32
        ).astype(jnp.bfloat16)

    dual = inverse(dual_modes)
    (gradient,) = by_radius(
        gradient_kernel, wet_mask, [heat_state, dual, *halo_planes(dual[-1:], dual[:1])], [jnp.float32]
    )
    new_state = inverse(forward_modes)
    radial_index = jnp.arange(radial, dtype=jnp.int32)[None, :, None]
    selected = jnp.where(radial_index == sensors[:, None, :], new_state, jnp.zeros_like(new_state))
    readings = jnp.sum(selected, axis=1)
    tangent_out = inverse(tangent_modes)
    return (new_state, tangent_out, gradient, readings)


def solution(mesh):
    def run(heat_state, tangent_in, cotangent, wet_mask, sensors, propagators):
        table = jnp.asarray(fourier_table(heat_state.shape[2]))
        field = P("depth", None, "azi")
        fits = mesh.shape["azi"] == 2 and mesh.shape["depth"] == 16
        body = fused_body if fits else split_body
        panel = P("depth", "azi")
        return jax.shard_map(
            body,
            mesh=mesh,
            in_specs=(P(), field, field, field, panel, panel, P("azi", "depth", None)),
            out_specs=(field, field, field, panel),
            check_vma=False,
        )(table, heat_state, tangent_in, cotangent, wet_mask, sensors, propagators)

    return run
```

```python
import functools
import math

import jax
import jax.numpy as jnp
import numpy as np
from jax import lax
from jax.experimental import pallas as pl
from jax.experimental.pallas import tpu as pltpu
from jax.sharding import PartitionSpec as P

mixing = 0.25
evaporation = 0.6
skin_depth = 16.0
mode_chunks = 2


def halo_planes(last, first):
    size = lax.axis_size("depth")
    up = [(i, i + 1) for i in range(size - 1)]
    down = [(j, i) for i, j in up]
    before = lax.ppermute(last, "depth", up)
    after = lax.ppermute(first, "depth", down)
    return before, after


def damping_profile(rows, lanes):
    radius = pl.program_id(0) * rows + lax.broadcasted_iota(jnp.int32, (rows, lanes), 0)
    return evaporation * jnp.exp(-radius.astype(jnp.float32) / skin_depth)


def plane(ref, before, after, z):
    source, index = (before, 0) if z < 0 else (after, 0) if z == ref.shape[0] else (ref, z)
    return source[index].astype(jnp.float32)


def mixed(ref, before, after, z):
    centre = plane(ref, before, after, z)
    around = plane(ref, before, after, z + 1) + plane(ref, before, after, z - 1)
    return centre, centre + mixing * (around - 2.0 * centre)


def rhs_kernel(wet, heat, heat_before, heat_after, tangent, tangent_before, tangent_after, out, tangent_out):
    slab, rows, lanes = heat.shape
    profile = damping_profile(rows, lanes)
    for z in range(slab):
        damping = wet[z : z + 1].astype(jnp.float32) * profile
        centre, value = mixed(heat, heat_before, heat_after, z)
        moisture = jnp.tanh(centre)
        out[z] = (value - damping * moisture).astype(out.dtype)
        slope = 1.0 - moisture * moisture
        centre, value = mixed(tangent, tangent_before, tangent_after, z)
        tangent_out[z] = (value - damping * slope * centre).astype(tangent_out.dtype)


def gradient_kernel(wet, heat, dual, dual_before, dual_after, out):
    slab, rows, lanes = heat.shape
    profile = damping_profile(rows, lanes)
    for z in range(slab):
        damping = wet[z : z + 1].astype(jnp.float32) * profile
        moisture = jnp.tanh(heat[z])
        slope = 1.0 - moisture * moisture
        centre, value = mixed(dual, dual_before, dual_after, z)
        out[z] = value - damping * slope * centre


def by_radius(kernel, wet, fields, dtypes):
    slab, radial, lanes = fields[0].shape
    rows = min(radial, 16)

    def spec(depth):
        return pl.BlockSpec((depth, rows, lanes), lambda i: (0, i, 0))

    count = len(dtypes) * slab * radial * lanes
    return pl.pallas_call(
        kernel,
        grid=(radial // rows,),
        in_specs=[pl.BlockSpec(wet.shape, lambda i: (0, 0))] + [spec(f.shape[0]) for f in fields],
        out_specs=[spec(slab) for _ in dtypes],
        out_shape=[jax.ShapeDtypeStruct((slab, radial, lanes), dtype) for dtype in dtypes],
        cost_estimate=pl.CostEstimate(flops=10 * count, bytes_accessed=6 * count, transcendentals=count),
    )(wet, *fields)


def fourier_table(length):
    wavenumber = np.arange(length, dtype=np.int32)[:, None]
    position = np.arange(length, dtype=np.int32)[None, :]
    midpoint = length // 2
    harmonic = np.where(wavenumber <= midpoint, wavenumber, wavenumber - midpoint)
    phase = (harmonic * position % length).astype(np.float32) * np.float32(2.0 * math.pi / length)
    waveform = np.where(wavenumber <= midpoint, np.cos(phase), np.sin(phase))
    boundary = (wavenumber == 0) | (wavenumber == midpoint)
    weights = np.where(boundary, math.sqrt(1.0 / length), math.sqrt(2.0 / length)).astype(np.float32)
    return (waveform * weights).astype(jnp.bfloat16)


def from_all(value):
    size = lax.axis_size("azi")
    blocks = [value]
    for shift in range(1, size):
        pairs = [(i, (i + shift) % size) for i in range(size)]
        blocks.append(lax.ppermute(value, "azi", pairs))
    return blocks


def split_body(table, heat_state, tangent_in, cotangent, wet_mask, sensors, propagators):
    slab, radial, local_azi = heat_state.shape
    size = lax.axis_size("azi")
    me = lax.axis_index("azi")
    owners = [lax.rem(me - shift + size, size) for shift in range(size)]
    modes = propagators.shape[0]
    step = modes // mode_chunks

    whole = [
        lax.all_gather(propagators[c * step : (c + 1) * step], "depth", axis=1, tiled=True)
        for c in range(mode_chunks)
    ]

    own_modes = lax.dynamic_slice_in_dim(table, me * modes, modes, axis=0)
    to_modes = [
        lax.dynamic_slice_in_dim(own_modes, owner * local_azi, local_azi, axis=1) for owner in owners
    ]
    own_azimuths = lax.dynamic_slice_in_dim(table, me * local_azi, local_azi, axis=1)
    to_azimuths = [
        lax.dynamic_slice_in_dim(own_azimuths, owner * modes, modes, axis=0) for owner in owners
    ]

    def part_spectrum(weights, block, c):
        return jnp.einsum(
            "ka,zra->kzr",
            weights[c * step : (c + 1) * step],
            block,
            preferred_element_type=jnp.float32,
        )

    seed_blocks = from_all(cotangent.astype(jnp.bfloat16))
    seed_part, heat_last, heat_first, tangent_last, tangent_first = lax.optimization_barrier(
        (
            part_spectrum(to_modes[0], seed_blocks[0], 0),
            heat_state[-1:],
            heat_state[:1],
            tangent_in[-1:],
            tangent_in[:1],
        )
    )

    forward_rhs, tangent_rhs = by_radius(
        rhs_kernel,
        wet_mask,
        [heat_state, *halo_planes(heat_last, heat_first), tangent_in, *halo_planes(tangent_last, tangent_first)],
        [jnp.bfloat16] * 2,
    )
    own_seed, forward_rhs, tangent_rhs = lax.optimization_barrier(
        (seed_blocks[0], forward_rhs, tangent_rhs)
    )
    seed_blocks = [own_seed] + seed_blocks[1:]
    forward_blocks = from_all(forward_rhs)
    tangent_blocks = from_all(tangent_rhs)

    def solve(blocks, formula, first=None):
        returned = []
        for c in range(mode_chunks):
            known = c == 0 and first is not None
            total = first if known else part_spectrum(to_modes[0], blocks[0], c)
            for weights, block in zip(to_modes[1:], blocks[1:]):
                total = total + part_spectrum(weights, block, c)
            solved = jnp.einsum(
                formula, whole[c], total.astype(jnp.bfloat16), preferred_element_type=jnp.float32
            ).astype(jnp.bfloat16)
            returned.append(from_all(solved))
        return returned

    def part_inverse(returned, pairs):
        total = 0.0
        for c, i in pairs:
            total = total + jnp.einsum(
                "ka,kzr->zra",
                to_azimuths[i][c * step : (c + 1) * step],
                returned[c][i],
                preferred_element_type=jnp.float32,
            )
        return total

    pairs = [(c, i) for i in range(size) for c in range(mode_chunks)]

    def inverse(returned):
        return part_inverse(returned, pairs).astype(jnp.bfloat16)

    dual_modes = solve(seed_blocks, "ksr,kzs->kzr", seed_part)
    dual_modes[0][0], *forward_received = lax.optimization_barrier(
        (dual_modes[0][0], *forward_blocks[1:])
    )
    forward_blocks = forward_blocks[:1] + forward_received
    forward_modes = solve(forward_blocks, "krs,kzs->kzr")
    tangent_modes = solve(tangent_blocks, "krs,kzs->kzr")

    dual = inverse(dual_modes)
    (gradient,) = by_radius(
        gradient_kernel, wet_mask, [heat_state, dual, *halo_planes(dual[-1:], dual[:1])], [jnp.float32]
    )

    new_state = inverse(forward_modes)
    radial_index = jnp.arange(radial, dtype=jnp.int32)[None, :, None]
    selected = jnp.where(radial_index == sensors[:, None, :], new_state, jnp.zeros_like(new_state))
    readings = jnp.sum(selected, axis=1)

    partial = part_inverse(tangent_modes, pairs[:-1])
    gradient, partial, tangent_modes[-1][-1] = lax.optimization_barrier(
        (gradient, partial, tangent_modes[-1][-1])
    )
    tangent_out = (partial + part_inverse(tangent_modes, pairs[-1:])).astype(jnp.bfloat16)
    return (new_state, tangent_out, gradient, readings)


fields = 3
parts = 8
early = parts // 2
bounds = (0, 2, 4, 6, 8, 10, 12, 13, 15, 16)
blocks = len(bounds) - 1
sections = ((0, 1, 2), (3, 4, 5), (6, 7, 8))
crossed = (7, 8)
own, other = 0, 1
ticks = 32


def timed(items):
    found = [[] for _ in range(ticks)]
    start = 0
    for item in items:
        found[start // 2].append(item)
        start += bounds[item[0] + 1] - bounds[item[0]]
    return found


def line_order():
    found = []
    for section in sections:
        group = [(q, c) for q in section for c in ((own, other) if q in crossed else (own,))]
        found += [(q, c, p) for p in range(3) for q, c in group]
    return timed(found)


def pair_order():
    found = []
    for section in sections:
        found += [(q, s) for s in range(4) for q in section if q not in crossed]
    found[10:10] = [(q, 0) for q in crossed]
    return timed(found)


def modes_kernel(
    shard, full, cotangent, heat, tangent, wet,
    out_seed, out_forward, out_tangent,
    matrices, table, values, stage, mine, theirs, given, raw, edges, damp,
    pair_send, pair_recv, up_send, up_recv, down_send, down_recv, azi_send, azi_recv,
    twin_send, twin_recv, back_send, back_recv, keep_sem, load_sem, table_sem, raw_sem, edge_send, edge_recv,
):
    outs = (out_seed, out_forward, out_tangent)
    flips = (True, False, False)
    place, azi = lax.axis_index("depth"), lax.axis_index("azi")
    z, x, core = place // 4, place // 2 % 2, place % 2
    pair, twin, up, down = place + 2 - 4 * x, place + 1 - 2 * core, place + 4, place - 4
    count, radial = matrices.shape[1], matrices.shape[3]
    step = count // parts
    fine = count // bounds[-1]
    half = count // 2
    chips = matrices.shape[0]
    slab = mine.shape[2]
    local = heat.shape[2]
    strip = raw.shape[3]
    strips = radial // strip
    last = lax.axis_size("depth") - 1
    planes = slab // parts
    mesh_ids = pl.DeviceIdType.MESH

    barrier = pltpu.get_barrier_semaphore()

    def greet(where, azimuth):
        pl.semaphore_signal(barrier, inc=1, device_id=(where, azimuth), device_id_type=mesh_ids)

    greet(pair, azi)
    greet(twin, azi)
    greet(place, 1 - azi)

    @pl.when(z < 3)
    def _():
        greet(up, azi)

    @pl.when(z > 0)
    def _():
        greet(down, azi)

    @pl.when(place < last)
    def _():
        greet(place + 1, azi)

    @pl.when(place > 0)
    def _():
        greet(place - 1, azi)

    inner = (place + last) // (last + 1) + (2 * last - place) // (last + 1)
    pl.semaphore_wait(barrier, 4 + (z + 1) // 2 % 2 + inner)

    def remote(src, dst, send, recv, where, azimuth=azi):
        return pltpu.make_async_remote_copy(
            src_ref=src, dst_ref=dst, send_sem=send, recv_sem=recv,
            device_id=(where, azimuth), device_id_type=mesh_ids,
        )

    def span_of(q):
        return pl.ds(bounds[q] * fine, (bounds[q + 1] - bounds[q]) * fine)

    def region(q, line, side):
        return matrices.at[2 * line + side, span_of(q)]

    flipped = (z, z + 1 - 2 * (z % 2), z + 2 - 4 * (z // 2), 3 - z)

    def pair_copy(q, s):
        ref = region(q, flipped[s], x)
        return remote(ref, ref, pair_send.at[q, s], pair_recv.at[q, s], pair)

    def line_item(q, c):
        return blocks + crossed.index(q) if c == other else q

    def up_copy(q, c, p):
        ref = region(q, z - p, x if c == own else 1 - x)
        k = line_item(q, c)
        return remote(ref, ref, up_send.at[k, p], up_recv.at[k, p], up)

    def down_copy(q, c, p):
        ref = region(q, z + p, x if c == own else 1 - x)
        k = line_item(q, c)
        return remote(ref, ref, down_send.at[k, p], down_recv.at[k, p], down)

    def azi_copy(n):
        if n < early:
            mine_at = matrices.at[2 * z + x, pl.ds(n * step, step)]
            theirs_at = matrices.at[2 * z + x, pl.ds(half + n * step, step)]
            return remote(mine_at, theirs_at, azi_send.at[n], azi_recv.at[n], place, 1 - azi)
        f, part = divmod(n - early, parts)
        span = planes * radial
        at = pl.ds(part * span, span)
        return remote(
            values.at[f, at, pl.ds(0, local)],
            values.at[f, at, pl.ds(local, local)],
            azi_send.at[n], azi_recv.at[n], place, 1 - azi,
        )

    pairs, lines, azis = pair_order(), line_order(), early + fields * parts

    lag, lead = 2, 2

    def each(t, act):
        if 0 <= t < ticks:
            for item in pairs[t]:
                act(pair_copy(*item))

    def azi_send_up_to(t):
        for n in range(0 if t == 0 else t + lead, min(t + lead + 1, azis)):
            azi_copy(n).start()

    def send(t):
        each(t, lambda copy: copy.start())
        azi_send_up_to(t)
        for q, c, p in lines[t] if t < ticks else ():

            @pl.when((z < 3) & (z >= p))
            def _():
                up_copy(q, c, p).start()

            @pl.when((z > 0) & (z + p <= 3))
            def _():
                down_copy(q, c, p).start()

    def receive(t):
        if t >= 0:
            for n in range(0 if t == 0 else t + lead, min(t + lead + 1, azis)):
                azi_copy(n).wait_recv()
        each(t, lambda copy: copy.wait_recv())
        for q, c, p in lines[t] if 0 <= t < ticks else ():

            @pl.when(z >= p + 1)
            def _():
                up_copy(q, c, p).wait_recv()

            @pl.when(z + p + 1 <= 3)
            def _():
                down_copy(q, c, p).wait_recv()

    def sent(t):
        each(t, lambda copy: copy.wait_send())
        if t < azis:
            azi_copy(t).wait_send()
        for q, c, p in lines[t]:

            @pl.when((z < 3) & (z >= p))
            def _():
                up_copy(q, c, p).wait_send()

            @pl.when((z > 0) & (z + p <= 3))
            def _():
                down_copy(q, c, p).wait_send()

    shard_load = pltpu.make_async_copy(
        shard, matrices.at[2 * z + x, pl.ds(0, half)], load_sem.at[0]
    )
    shard_load.start()
    damp_load = pltpu.make_async_copy(wet, damp, load_sem.at[1])
    damp_load.start()

    def strip_loads(n):
        slot = n % 2
        c = n % strips
        span = pl.ds(c * strip, strip)
        if n < strips:
            return [
                pltpu.make_async_copy(
                    cotangent.at[:, span, :], raw.at[slot, 0, pl.ds(1, slab)], raw_sem.at[slot, 0]
                )
            ]
        found = []
        for f, source in enumerate((heat, tangent)):
            found.append((source.at[:, span, :], raw.at[slot, f, pl.ds(1, slab)], 3 * f))
            found.append((edges.at[f, 0, span], raw.at[slot, f, 0], 3 * f + 1))
            found.append((edges.at[f, 1, span], raw.at[slot, f, slab + 1], 3 * f + 2))
        return [pltpu.make_async_copy(a, b, raw_sem.at[slot, i]) for a, b, i in found]

    for load in strip_loads(0):
        load.start()

    def edge_copies(side):
        out = []
        for f, source in enumerate((heat, tangent)):
            out.append(
                remote(
                    source.at[slab - 1 if side == 0 else 0], edges.at[f, side],
                    edge_send.at[f, side], edge_recv.at[f, side],
                    place + 1 if side == 0 else place - 1,
                )
            )
        return out

    def edges_out():
        @pl.when(place < last)
        def _():
            for copy in edge_copies(0):
                copy.start()

        @pl.when(place > 0)
        def _():
            for copy in edge_copies(1):
                copy.start()

    def edges_in():
        for side, empty, full_side in ((0, place == 0, place > 0), (1, place == last, place < last)):

            @pl.when(full_side)
            def _():
                for copy in edge_copies(side):
                    copy.wait_recv()

            @pl.when(empty)
            def _():
                edges[:, side] = jnp.zeros((2, radial, local), jnp.float32)

    def edges_sent():
        @pl.when(place < last)
        def _():
            for copy in edge_copies(0):
                copy.wait_send()

        @pl.when(place > 0)
        def _():
            for copy in edge_copies(1):
                copy.wait_send()

    table_loads = []
    for part in range(4):
        owner, which = (azi, 1 - azi)[part % 2], (1 - core, core)[part // 2]
        row = pl.multiple_of((2 * owner + which) * (half), half)
        for h in range(2):
            col = pl.multiple_of((azi, 1 - azi)[h] * local, local)
            table_loads.append(
                pltpu.make_async_copy(
                    full.at[pl.ds(row, half), pl.ds(col, local)],
                    table.at[pl.ds(part * half, half), pl.ds(h * local, local)],
                    table_sem.at[part, h],
                )
            )

    def prepare(n):
        slot = n % 2
        c = n % strips
        if n + 1 == strips:
            edges_in()
        if n + 1 < 2 * strips:
            for load in strip_loads(n + 1):
                load.start()
        for load in strip_loads(n):
            load.wait()
        radius = c * strip + lax.broadcasted_iota(jnp.int32, (strip, local), 0)
        profile = evaporation * jnp.exp(-radius.astype(jnp.float32) / skin_depth)

        def plane_step(p, _):
            into = pl.ds(pl.multiple_of(p * radial + c * strip, strip), strip)
            if n < strips:
                values[0, into, pl.ds(0, local)] = raw[slot, 0, p + 1].astype(jnp.bfloat16)
                return 0
            damping = damp[pl.ds(p, 1), :].astype(jnp.float32) * profile

            def mix(f):
                centre = raw[slot, f, p + 1]
                around = raw[slot, f, p + 2] + raw[slot, f, p]
                return centre, centre + mixing * (around - 2.0 * centre)

            centre, value = mix(0)
            moisture = jnp.tanh(centre)
            values[1, into, pl.ds(0, local)] = (value - damping * moisture).astype(jnp.bfloat16)
            slope = 1.0 - moisture * moisture
            centre, value = mix(1)
            values[2, into, pl.ds(0, local)] = (value - damping * slope * centre).astype(jnp.bfloat16)
            return 0

        lax.fori_loop(0, slab, plane_step, 0)

    def twin_copy(f, part):
        at = pl.ds(part * half, half)
        return remote(
            given.at[f % 2, at], theirs.at[f, at], twin_send.at[f, part], twin_recv.at[f, part], twin
        )

    group = 4

    def transform(f, n):
        span = group * radial
        cols = values[f, pl.ds(n * span, span), :]

        def half_step(h, _):
            weights = table[pl.ds(pl.multiple_of(h * count, count), count), :]
            out = lax.dot_general(
                weights, cols, (((1,), (1,)), ((), ())), preferred_element_type=jnp.float32
            )
            for g in range(group):
                at = pl.multiple_of((n * group + g) * 2 * count + h * count, count)
                stage[pl.ds(at, count), :] = out[:, g * radial : (g + 1) * radial]
            return 0

        lax.fori_loop(0, 2, half_step, 0)

    def turn(into, f, first, begin, end):
        def one(n, _):
            for u in range(8):
                k = n * 8 + u
                into[f, k] = stage[pl.ds(first + k, slab, stride=2 * count), :].astype(jnp.bfloat16)
            return 0

        lax.fori_loop(begin // 8, end // 8, one, 0)

    def give(f):
        for part in range(2):
            if f == 2:
                twin_copy(0, part).wait_send()
            turn(given, f % 2, 0, part * half, (part + 1) * half)
            twin_copy(f, part).start()

    def take(f):
        turn(mine, f, count, 0, count)

    def keep_copy(f, q):
        at = span_of(q)
        return pltpu.make_async_copy(mine.at[f, at], outs[f].at[at], keep_sem.at[f, q])

    def back_copy(f, q):
        return remote(
            theirs.at[f, span_of(q)],
            outs[f].at[pl.ds(count + bounds[q] * fine, (bounds[q + 1] - bounds[q]) * fine)],
            back_send.at[f, q], back_recv.at[f, q], twin,
        )

    def solve(which, q):
        def one(n, _):
            found = []
            for u in range(16):
                k = bounds[q] * fine + n * 16 + u
                matrix = jnp.concatenate([matrices[c, k] for c in range(chips)], axis=0)
                for flip in (True, False):
                    chosen = [f for f in which if flips[f] == flip]
                    if not chosen:
                        continue
                    stacked = jnp.concatenate(
                        [part[f, k] for f in chosen for part in (mine, theirs)], axis=0
                    )
                    out = lax.dot_general(
                        stacked, matrix, (((1,), (0 if flip else 1,)), ((), ())),
                        preferred_element_type=jnp.float32,
                    )
                    found.append((chosen, k, out))
            for chosen, k, out in found:
                out = out.astype(jnp.bfloat16)
                for i, f in enumerate(chosen):
                    mine[f, k] = out[2 * i * slab : (2 * i + 1) * slab]
                    theirs[f, k] = out[(2 * i + 1) * slab : (2 * i + 2) * slab]
            return 0

        lax.fori_loop(0, (bounds[q + 1] - bounds[q]) * fine // 16, one, 0)
        for f in which:
            keep_copy(f, q).start()
            back_copy(f, q).start()

    def met(f):
        for part in range(2):
            twin_copy(f, part).wait_recv()

    def begin():
        edges_out()
        for load in table_loads:
            load.start()
        damp_load.wait()
        for n in range(4):
            prepare(n)

    def table_in():
        for load in table_loads:
            load.wait()

    P = functools.partial
    tasks = {0: [begin], 1: [P(prepare, n) for n in range(4, strips)], 2: [table_in]}
    for n in range(strips):
        tasks.setdefault(2 + n, []).append(P(prepare, strips + n))
    for f in range(fields):
        for n in range(slab // group):
            ready = early + f * parts + (n + 1) * group // planes - 1
            tasks.setdefault(ready, []).append(P(transform, f, n))
    more = {
        11: [P(give, 0), P(take, 0)],
        13: [P(met, 0), P(solve, [0], 0)],
        14: [P(solve, [0], 1)],
        15: [P(solve, [0], 2)],
        19: [P(give, 1), P(take, 1)],
        21: [P(met, 1), P(solve, [1], 0)],
        22: [P(solve, [1], 1), P(solve, [1], 2)],
        24: [P(solve, [0, 1], 3)],
        25: [P(solve, [0, 1], 4)],
        26: [P(solve, [0, 1], 5)],
        27: [P(give, 2), P(take, 2)],
        28: [P(solve, [0, 1], 7), P(met, 2)] + [P(solve, [2], q) for q in (0, 1, 2, 3, 4, 5, 7)],
        29: [P(solve, [0, 1, 2], 6)],
        30: [P(solve, [0, 1, 2], 8)],
    }
    for t, found in more.items():
        tasks.setdefault(t, []).extend(found)

    shard_load.wait()
    for t in range(ticks - 1):
        receive(t - lag)
        send(t)
        for task in tasks.get(t, []):
            task()

    edges_sent()
    for t in range(ticks - 1):
        sent(t)
    for f in range(fields):
        for part in range(2):
            if f > 0:
                twin_copy(f, part).wait_send()
        for q in range(blocks):
            keep_copy(f, q).wait()
            back_copy(f, q).wait()


def solved_modes(shard, table, cotangent, heat, tangent, wet):
    slab, radial, local = heat.shape
    half, rows, _ = shard.shape
    count = 2 * half
    strip = 16
    dma = pltpu.SemaphoreType.DMA
    out = jax.ShapeDtypeStruct((2 * count, slab, radial), jnp.bfloat16)
    modes = pltpu.VMEM((fields, count, slab, radial), jnp.bfloat16)
    return pl.pallas_call(
        modes_kernel,
        out_shape=[out] * fields,
        in_specs=[pl.BlockSpec(memory_space=pl.ANY)] * 6,
        out_specs=[pl.BlockSpec(memory_space=pl.ANY)] * fields,
        scratch_shapes=[
            pltpu.VMEM((radial // rows, count, rows, radial), jnp.bfloat16),
            pltpu.VMEM((2 * count, 2 * local), jnp.bfloat16),
            pltpu.VMEM((fields, slab * radial, 2 * local), jnp.bfloat16),
            pltpu.VMEM((2 * slab * count, radial), jnp.float32),
            modes,
            modes,
            pltpu.VMEM((2, count, slab, radial), jnp.bfloat16),
            pltpu.VMEM((2, 2, slab + 2, strip, local), jnp.float32),
            pltpu.VMEM((2, 2, radial, local), jnp.float32),
            pltpu.VMEM((slab, local), jnp.int32),
            dma((blocks, 4)), dma((blocks, 4)),
            dma((blocks + len(crossed), 3)), dma((blocks + len(crossed), 3)),
            dma((blocks + len(crossed), 3)), dma((blocks + len(crossed), 3)),
            dma((early + fields * parts,)), dma((early + fields * parts,)),
            dma((fields, 2)), dma((fields, 2)),
            dma((fields, blocks)), dma((fields, blocks)), dma((fields, blocks)),
            dma((2,)), dma((4, 2)), dma((2, 6)), dma((2, 2)), dma((2, 2)),
        ],
        compiler_params=pltpu.CompilerParams(
            collective_id=0, has_side_effects=True, vmem_limit_bytes=62 * 1024 * 1024
        ),
        cost_estimate=pl.CostEstimate(flops=15 * 10**9, bytes_accessed=10**8, transcendentals=0),
    )(shard, table, cotangent, heat, tangent, wet)


def fused_body(table, heat_state, tangent_in, cotangent, wet_mask, sensors, propagators):
    slab, radial, local_azi = heat_state.shape
    depth = lax.axis_size("depth")
    me = lax.axis_index("azi")
    core = lax.rem(lax.axis_index("depth"), 2)
    modes = propagators.shape[0]
    half = modes // 2

    mine = lax.dynamic_slice_in_dim(propagators, core * half, half, axis=0)
    outgoing = lax.dynamic_slice_in_dim(propagators, (1 - core) * half, half, axis=0)
    incoming = lax.ppermute(outgoing, "depth", [(i, i ^ 1) for i in range(depth)])
    shard = jnp.concatenate(
        [jnp.where(core == 0, mine, incoming), jnp.where(core == 0, incoming, mine)], axis=1
    )

    def table_rows(which):
        return [
            lax.dynamic_slice_in_dim(table, owner * modes + which * half, half, axis=0)
            for owner in (me, 1 - me)
        ]

    own_rows = jnp.concatenate(table_rows(core), axis=0)
    twin_rows = jnp.concatenate(table_rows(1 - core), axis=0)

    def columns(weights, owner):
        return lax.dynamic_slice_in_dim(weights, owner * local_azi, local_azi, axis=1)

    to_azimuths = columns(jnp.concatenate([own_rows, twin_rows], axis=0), me)

    dual_modes, forward_modes, tangent_modes = solved_modes(
        shard, table, cotangent, heat_state, tangent_in, wet_mask
    )

    def inverse(solved):
        return jnp.einsum(
            "ka,kzr->zra", to_azimuths, solved, preferred_element_type=jnp.float32
        ).astype(jnp.bfloat16)

    dual = inverse(dual_modes)
    (gradient,) = by_radius(
        gradient_kernel, wet_mask, [heat_state, dual, *halo_planes(dual[-1:], dual[:1])], [jnp.float32]
    )
    new_state = inverse(forward_modes)
    radial_index = jnp.arange(radial, dtype=jnp.int32)[None, :, None]
    selected = jnp.where(radial_index == sensors[:, None, :], new_state, jnp.zeros_like(new_state))
    readings = jnp.sum(selected, axis=1)
    tangent_out = inverse(tangent_modes)
    return (new_state, tangent_out, gradient, readings)


def solution(mesh):
    def run(heat_state, tangent_in, cotangent, wet_mask, sensors, propagators):
        table = jnp.asarray(fourier_table(heat_state.shape[2]))
        field = P("depth", None, "azi")
        fits = mesh.shape["azi"] == 2 and mesh.shape["depth"] == 16
        body = fused_body if fits else split_body
        panel = P("depth", "azi")
        return jax.shard_map(
            body,
            mesh=mesh,
            in_specs=(P(), field, field, field, panel, panel, P("azi", "depth", None)),
            out_specs=(field, field, field, panel),
            check_vma=False,
        )(table, heat_state, tangent_in, cotangent, wet_mask, sensors, propagators)

    return run
```

```python
import functools
import math

import jax
import jax.numpy as jnp
import numpy as np
from jax import lax
from jax.experimental import pallas as pl
from jax.experimental.pallas import tpu as pltpu
from jax.sharding import PartitionSpec as P

mixing = 0.25
evaporation = 0.6
skin_depth = 16.0
mode_chunks = 2


def halo_planes(last, first):
    size = lax.axis_size("depth")
    up = [(i, i + 1) for i in range(size - 1)]
    down = [(j, i) for i, j in up]
    before = lax.ppermute(last, "depth", up)
    after = lax.ppermute(first, "depth", down)
    return before, after


def damping_profile(rows, lanes):
    radius = pl.program_id(0) * rows + lax.broadcasted_iota(jnp.int32, (rows, lanes), 0)
    return evaporation * jnp.exp(-radius.astype(jnp.float32) / skin_depth)


def plane(ref, before, after, z):
    source, index = (before, 0) if z < 0 else (after, 0) if z == ref.shape[0] else (ref, z)
    return source[index].astype(jnp.float32)


def mixed(ref, before, after, z):
    centre = plane(ref, before, after, z)
    around = plane(ref, before, after, z + 1) + plane(ref, before, after, z - 1)
    return centre, centre + mixing * (around - 2.0 * centre)


def rhs_kernel(wet, heat, heat_before, heat_after, tangent, tangent_before, tangent_after, out, tangent_out):
    slab, rows, lanes = heat.shape
    profile = damping_profile(rows, lanes)
    for z in range(slab):
        damping = wet[z : z + 1].astype(jnp.float32) * profile
        centre, value = mixed(heat, heat_before, heat_after, z)
        moisture = jnp.tanh(centre)
        out[z] = (value - damping * moisture).astype(out.dtype)
        slope = 1.0 - moisture * moisture
        centre, value = mixed(tangent, tangent_before, tangent_after, z)
        tangent_out[z] = (value - damping * slope * centre).astype(tangent_out.dtype)


def gradient_kernel(wet, heat, dual, dual_before, dual_after, out):
    slab, rows, lanes = heat.shape
    profile = damping_profile(rows, lanes)
    for z in range(slab):
        damping = wet[z : z + 1].astype(jnp.float32) * profile
        moisture = jnp.tanh(heat[z])
        slope = 1.0 - moisture * moisture
        centre, value = mixed(dual, dual_before, dual_after, z)
        out[z] = value - damping * slope * centre


def by_radius(kernel, wet, fields, dtypes):
    slab, radial, lanes = fields[0].shape
    rows = min(radial, 16)

    def spec(depth):
        return pl.BlockSpec((depth, rows, lanes), lambda i: (0, i, 0))

    count = len(dtypes) * slab * radial * lanes
    return pl.pallas_call(
        kernel,
        grid=(radial // rows,),
        in_specs=[pl.BlockSpec(wet.shape, lambda i: (0, 0))] + [spec(f.shape[0]) for f in fields],
        out_specs=[spec(slab) for _ in dtypes],
        out_shape=[jax.ShapeDtypeStruct((slab, radial, lanes), dtype) for dtype in dtypes],
        cost_estimate=pl.CostEstimate(flops=10 * count, bytes_accessed=6 * count, transcendentals=count),
    )(wet, *fields)


def fourier_table(length):
    wavenumber = np.arange(length, dtype=np.int32)[:, None]
    position = np.arange(length, dtype=np.int32)[None, :]
    midpoint = length // 2
    harmonic = np.where(wavenumber <= midpoint, wavenumber, wavenumber - midpoint)
    phase = (harmonic * position % length).astype(np.float32) * np.float32(2.0 * math.pi / length)
    waveform = np.where(wavenumber <= midpoint, np.cos(phase), np.sin(phase))
    boundary = (wavenumber == 0) | (wavenumber == midpoint)
    weights = np.where(boundary, math.sqrt(1.0 / length), math.sqrt(2.0 / length)).astype(np.float32)
    return (waveform * weights).astype(jnp.bfloat16)


def from_all(value):
    size = lax.axis_size("azi")
    blocks = [value]
    for shift in range(1, size):
        pairs = [(i, (i + shift) % size) for i in range(size)]
        blocks.append(lax.ppermute(value, "azi", pairs))
    return blocks


def split_body(table, heat_state, tangent_in, cotangent, wet_mask, sensors, propagators):
    slab, radial, local_azi = heat_state.shape
    size = lax.axis_size("azi")
    me = lax.axis_index("azi")
    owners = [lax.rem(me - shift + size, size) for shift in range(size)]
    modes = propagators.shape[0]
    step = modes // mode_chunks

    whole = [
        lax.all_gather(propagators[c * step : (c + 1) * step], "depth", axis=1, tiled=True)
        for c in range(mode_chunks)
    ]

    own_modes = lax.dynamic_slice_in_dim(table, me * modes, modes, axis=0)
    to_modes = [
        lax.dynamic_slice_in_dim(own_modes, owner * local_azi, local_azi, axis=1) for owner in owners
    ]
    own_azimuths = lax.dynamic_slice_in_dim(table, me * local_azi, local_azi, axis=1)
    to_azimuths = [
        lax.dynamic_slice_in_dim(own_azimuths, owner * modes, modes, axis=0) for owner in owners
    ]

    def part_spectrum(weights, block, c):
        return jnp.einsum(
            "ka,zra->kzr",
            weights[c * step : (c + 1) * step],
            block,
            preferred_element_type=jnp.float32,
        )

    seed_blocks = from_all(cotangent.astype(jnp.bfloat16))
    seed_part, heat_last, heat_first, tangent_last, tangent_first = lax.optimization_barrier(
        (
            part_spectrum(to_modes[0], seed_blocks[0], 0),
            heat_state[-1:],
            heat_state[:1],
            tangent_in[-1:],
            tangent_in[:1],
        )
    )

    forward_rhs, tangent_rhs = by_radius(
        rhs_kernel,
        wet_mask,
        [heat_state, *halo_planes(heat_last, heat_first), tangent_in, *halo_planes(tangent_last, tangent_first)],
        [jnp.bfloat16] * 2,
    )
    own_seed, forward_rhs, tangent_rhs = lax.optimization_barrier(
        (seed_blocks[0], forward_rhs, tangent_rhs)
    )
    seed_blocks = [own_seed] + seed_blocks[1:]
    forward_blocks = from_all(forward_rhs)
    tangent_blocks = from_all(tangent_rhs)

    def solve(blocks, formula, first=None):
        returned = []
        for c in range(mode_chunks):
            known = c == 0 and first is not None
            total = first if known else part_spectrum(to_modes[0], blocks[0], c)
            for weights, block in zip(to_modes[1:], blocks[1:]):
                total = total + part_spectrum(weights, block, c)
            solved = jnp.einsum(
                formula, whole[c], total.astype(jnp.bfloat16), preferred_element_type=jnp.float32
            ).astype(jnp.bfloat16)
            returned.append(from_all(solved))
        return returned

    def part_inverse(returned, pairs):
        total = 0.0
        for c, i in pairs:
            total = total + jnp.einsum(
                "ka,kzr->zra",
                to_azimuths[i][c * step : (c + 1) * step],
                returned[c][i],
                preferred_element_type=jnp.float32,
            )
        return total

    pairs = [(c, i) for i in range(size) for c in range(mode_chunks)]

    def inverse(returned):
        return part_inverse(returned, pairs).astype(jnp.bfloat16)

    dual_modes = solve(seed_blocks, "ksr,kzs->kzr", seed_part)
    dual_modes[0][0], *forward_received = lax.optimization_barrier(
        (dual_modes[0][0], *forward_blocks[1:])
    )
    forward_blocks = forward_blocks[:1] + forward_received
    forward_modes = solve(forward_blocks, "krs,kzs->kzr")
    tangent_modes = solve(tangent_blocks, "krs,kzs->kzr")

    dual = inverse(dual_modes)
    (gradient,) = by_radius(
        gradient_kernel, wet_mask, [heat_state, dual, *halo_planes(dual[-1:], dual[:1])], [jnp.float32]
    )

    new_state = inverse(forward_modes)
    radial_index = jnp.arange(radial, dtype=jnp.int32)[None, :, None]
    selected = jnp.where(radial_index == sensors[:, None, :], new_state, jnp.zeros_like(new_state))
    readings = jnp.sum(selected, axis=1)

    partial = part_inverse(tangent_modes, pairs[:-1])
    gradient, partial, tangent_modes[-1][-1] = lax.optimization_barrier(
        (gradient, partial, tangent_modes[-1][-1])
    )
    tangent_out = (partial + part_inverse(tangent_modes, pairs[-1:])).astype(jnp.bfloat16)
    return (new_state, tangent_out, gradient, readings)


fields = 3
parts = 8
early = parts // 2
bounds = (0, 2, 4, 6, 8, 10, 12, 13, 15, 16)
blocks = len(bounds) - 1
sections = ((0, 1, 2), (3, 4, 5), (6, 7, 8))
crossed = (7, 8)
order = (1, 2, 0)
own, other = 0, 1
ticks = 32


def timed(items):
    found = [[] for _ in range(ticks)]
    start = 0
    for item in items:
        found[start // 2].append(item)
        start += bounds[item[0] + 1] - bounds[item[0]]
    return found


def line_order():
    found = []
    for section in sections:
        group = [(q, c) for q in section for c in ((own, other) if q in crossed else (own,))]
        found += [(q, c, p) for p in range(3) for q, c in group]
    return timed(found)


def pair_order():
    found = []
    for section in sections:
        found += [(q, s) for s in range(4) for q in section if q not in crossed]
    found[10:10] = [(q, 0) for q in crossed]
    return timed(found)


def modes_kernel(
    shard, full, cotangent, heat, tangent, wet,
    out_seed, out_forward, out_tangent,
    matrices, table, values, stage, mine, theirs, given, raw, edges, damp,
    pair_send, pair_recv, up_send, up_recv, down_send, down_recv, azi_send, azi_recv,
    twin_send, twin_recv, back_send, back_recv, keep_sem, load_sem, table_sem, raw_sem, edge_send, edge_recv,
):
    outs = (out_seed, out_forward, out_tangent)
    flips = (True, False, False)
    place, azi = lax.axis_index("depth"), lax.axis_index("azi")
    z, x, core = place // 4, place // 2 % 2, place % 2
    pair, twin, up, down = place + 2 - 4 * x, place + 1 - 2 * core, place + 4, place - 4
    count, radial = matrices.shape[1], matrices.shape[3]
    step = count // parts
    fine = count // bounds[-1]
    half = count // 2
    chips = matrices.shape[0]
    slab = mine.shape[2]
    local = heat.shape[2]
    strip = raw.shape[3]
    strips = radial // strip
    last = lax.axis_size("depth") - 1
    planes = slab // parts
    mesh_ids = pl.DeviceIdType.MESH

    barrier = pltpu.get_barrier_semaphore()

    def greet(where, azimuth):
        pl.semaphore_signal(barrier, inc=1, device_id=(where, azimuth), device_id_type=mesh_ids)

    greet(pair, azi)
    greet(twin, azi)
    greet(place, 1 - azi)

    @pl.when(z < 3)
    def _():
        greet(up, azi)

    @pl.when(z > 0)
    def _():
        greet(down, azi)

    @pl.when(place < last)
    def _():
        greet(place + 1, azi)

    @pl.when(place > 0)
    def _():
        greet(place - 1, azi)

    inner = (place + last) // (last + 1) + (2 * last - place) // (last + 1)
    pl.semaphore_wait(barrier, 4 + (z + 1) // 2 % 2 + inner)

    def remote(src, dst, send, recv, where, azimuth=azi):
        return pltpu.make_async_remote_copy(
            src_ref=src, dst_ref=dst, send_sem=send, recv_sem=recv,
            device_id=(where, azimuth), device_id_type=mesh_ids,
        )

    def span_of(q):
        return pl.ds(bounds[q] * fine, (bounds[q + 1] - bounds[q]) * fine)

    def region(q, line, side):
        return matrices.at[2 * line + side, span_of(q)]

    flipped = (z, z + 1 - 2 * (z % 2), z + 2 - 4 * (z // 2), 3 - z)

    def pair_copy(q, s):
        ref = region(q, flipped[s], x)
        return remote(ref, ref, pair_send.at[q, s], pair_recv.at[q, s], pair)

    def line_item(q, c):
        return blocks + crossed.index(q) if c == other else q

    def up_copy(q, c, p):
        ref = region(q, z - p, x if c == own else 1 - x)
        k = line_item(q, c)
        return remote(ref, ref, up_send.at[k, p], up_recv.at[k, p], up)

    def down_copy(q, c, p):
        ref = region(q, z + p, x if c == own else 1 - x)
        k = line_item(q, c)
        return remote(ref, ref, down_send.at[k, p], down_recv.at[k, p], down)

    def azi_copy(n):
        if n < early:
            mine_at = matrices.at[2 * z + x, pl.ds(n * step, step)]
            theirs_at = matrices.at[2 * z + x, pl.ds(half + n * step, step)]
            return remote(mine_at, theirs_at, azi_send.at[n], azi_recv.at[n], place, 1 - azi)
        turn_of, part = divmod(n - early, parts)
        f = order[turn_of]
        span = planes * radial
        at = pl.ds(part * span, span)
        return remote(
            values.at[f, at, pl.ds(0, local)],
            values.at[f, at, pl.ds(local, local)],
            azi_send.at[n], azi_recv.at[n], place, 1 - azi,
        )

    pairs, lines, azis = pair_order(), line_order(), early + fields * parts

    lag, lead = 2, 4

    def each(t, act):
        if 0 <= t < ticks:
            for item in pairs[t]:
                act(pair_copy(*item))

    def azi_until(t):
        return early if t < 2 else min(t + lead + 1, azis)

    def azi_send_up_to(t):
        for n in range(0 if t == 0 else azi_until(t - 1), azi_until(t)):
            azi_copy(n).start()

    def azi_in(begin, end):
        for n in range(begin, end):
            azi_copy(n).wait_recv()

    def send(t):
        each(t, lambda copy: copy.start())
        azi_send_up_to(t)
        for q, c, p in lines[t] if t < ticks else ():

            @pl.when((z < 3) & (z >= p))
            def _():
                up_copy(q, c, p).start()

            @pl.when((z > 0) & (z + p <= 3))
            def _():
                down_copy(q, c, p).start()

    def receive(t):
        if t == early:
            azi_in(0, early)
        each(t, lambda copy: copy.wait_recv())
        for q, c, p in lines[t] if 0 <= t < ticks else ():

            @pl.when(z >= p + 1)
            def _():
                up_copy(q, c, p).wait_recv()

            @pl.when(z + p + 1 <= 3)
            def _():
                down_copy(q, c, p).wait_recv()

    def sent(t):
        each(t, lambda copy: copy.wait_send())
        if t < azis:
            azi_copy(t).wait_send()
        for q, c, p in lines[t]:

            @pl.when((z < 3) & (z >= p))
            def _():
                up_copy(q, c, p).wait_send()

            @pl.when((z > 0) & (z + p <= 3))
            def _():
                down_copy(q, c, p).wait_send()

    shard_load = pltpu.make_async_copy(
        shard, matrices.at[2 * z + x, pl.ds(0, half)], load_sem.at[0]
    )
    shard_load.start()
    damp_load = pltpu.make_async_copy(wet, damp, load_sem.at[1])
    damp_load.start()

    def strip_loads(n):
        slot = n % 2
        c = n % strips
        span = pl.ds(c * strip, strip)
        if n >= strips:
            return [
                pltpu.make_async_copy(
                    cotangent.at[:, span, :], raw.at[slot, 0, pl.ds(1, slab)], raw_sem.at[slot, 0]
                )
            ]
        found = []
        for f, source in enumerate((heat, tangent)):
            found.append((source.at[:, span, :], raw.at[slot, f, pl.ds(1, slab)], 3 * f))
            found.append((edges.at[f, 0, span], raw.at[slot, f, 0], 3 * f + 1))
            found.append((edges.at[f, 1, span], raw.at[slot, f, slab + 1], 3 * f + 2))
        return [pltpu.make_async_copy(a, b, raw_sem.at[slot, i]) for a, b, i in found]

    def edge_copies(side):
        out = []
        for f, source in enumerate((heat, tangent)):
            out.append(
                remote(
                    source.at[slab - 1 if side == 0 else 0], edges.at[f, side],
                    edge_send.at[f, side], edge_recv.at[f, side],
                    place + 1 if side == 0 else place - 1,
                )
            )
        return out

    def edges_out():
        @pl.when(place < last)
        def _():
            for copy in edge_copies(0):
                copy.start()

        @pl.when(place > 0)
        def _():
            for copy in edge_copies(1):
                copy.start()

    def edges_in():
        for side, empty, full_side in ((0, place == 0, place > 0), (1, place == last, place < last)):

            @pl.when(full_side)
            def _():
                for copy in edge_copies(side):
                    copy.wait_recv()

            @pl.when(empty)
            def _():
                edges[:, side] = jnp.zeros((2, radial, local), jnp.float32)

    def edges_sent():
        @pl.when(place < last)
        def _():
            for copy in edge_copies(0):
                copy.wait_send()

        @pl.when(place > 0)
        def _():
            for copy in edge_copies(1):
                copy.wait_send()

    table_loads = []
    for part in range(4):
        owner, which = (azi, 1 - azi)[part % 2], (1 - core, core)[part // 2]
        row = pl.multiple_of((2 * owner + which) * (half), half)
        for h in range(2):
            col = pl.multiple_of((azi, 1 - azi)[h] * local, local)
            table_loads.append(
                pltpu.make_async_copy(
                    full.at[pl.ds(row, half), pl.ds(col, local)],
                    table.at[pl.ds(part * half, half), pl.ds(h * local, local)],
                    table_sem.at[part, h],
                )
            )

    def prepare(n):
        slot = n % 2
        c = n % strips
        if n + 1 < 2 * strips:
            for load in strip_loads(n + 1):
                load.start()
        for load in strip_loads(n):
            load.wait()
        radius = c * strip + lax.broadcasted_iota(jnp.int32, (strip, local), 0)
        profile = evaporation * jnp.exp(-radius.astype(jnp.float32) / skin_depth)

        def plane_step(p, _):
            into = pl.ds(pl.multiple_of(p * radial + c * strip, strip), strip)
            if n >= strips:
                values[0, into, pl.ds(0, local)] = raw[slot, 0, p + 1].astype(jnp.bfloat16)
                return 0
            damping = damp[pl.ds(p, 1), :].astype(jnp.float32) * profile

            def mix(f):
                centre = raw[slot, f, p + 1]
                around = raw[slot, f, p + 2] + raw[slot, f, p]
                return centre, centre + mixing * (around - 2.0 * centre)

            centre, value = mix(0)
            moisture = jnp.tanh(centre)
            values[1, into, pl.ds(0, local)] = (value - damping * moisture).astype(jnp.bfloat16)
            slope = 1.0 - moisture * moisture
            centre, value = mix(1)
            values[2, into, pl.ds(0, local)] = (value - damping * slope * centre).astype(jnp.bfloat16)
            return 0

        lax.fori_loop(0, slab, plane_step, 0)

    def twin_copy(f, part):
        at = pl.ds(part * half, half)
        return remote(
            given.at[order.index(f) % 2, at], theirs.at[f, at], twin_send.at[f, part], twin_recv.at[f, part], twin
        )

    group = 4

    def transform(f, n):
        span = group * radial
        cols = values[f, pl.ds(n * span, span), :]

        def half_step(h, _):
            weights = table[pl.ds(pl.multiple_of(h * count, count), count), :]
            out = lax.dot_general(
                weights, cols, (((1,), (1,)), ((), ())), preferred_element_type=jnp.float32
            )
            for g in range(group):
                at = pl.multiple_of((n * group + g) * 2 * count + h * count, count)
                stage[pl.ds(at, count), :] = out[:, g * radial : (g + 1) * radial]
            return 0

        lax.fori_loop(0, 2, half_step, 0)

    def turn(into, f, first, begin, end):
        def one(n, _):
            for u in range(8):
                k = n * 8 + u
                into[f, k] = stage[pl.ds(first + k, slab, stride=2 * count), :].astype(jnp.bfloat16)
            return 0

        lax.fori_loop(begin // 8, end // 8, one, 0)

    def give(f):
        for part in range(2):
            if f == order[2]:
                twin_copy(order[0], part).wait_send()
            turn(given, order.index(f) % 2, 0, part * half, (part + 1) * half)
            twin_copy(f, part).start()

    def take(f):
        turn(mine, f, count, 0, count)

    def keep_copy(f, q):
        at = span_of(q)
        return pltpu.make_async_copy(mine.at[f, at], outs[f].at[at], keep_sem.at[f, q])

    def back_copy(f, q):
        return remote(
            theirs.at[f, span_of(q)],
            outs[f].at[pl.ds(count + bounds[q] * fine, (bounds[q + 1] - bounds[q]) * fine)],
            back_send.at[f, q], back_recv.at[f, q], twin,
        )

    def solve(which, q):
        def one(n, _):
            found = []
            for u in range(16):
                k = bounds[q] * fine + n * 16 + u
                matrix = jnp.concatenate([matrices[c, k] for c in range(chips)], axis=0)
                for flip in (True, False):
                    chosen = [f for f in which if flips[f] == flip]
                    if not chosen:
                        continue
                    stacked = jnp.concatenate(
                        [part[f, k] for f in chosen for part in (mine, theirs)], axis=0
                    )
                    out = lax.dot_general(
                        stacked, matrix, (((1,), (0 if flip else 1,)), ((), ())),
                        preferred_element_type=jnp.float32,
                    )
                    found.append((chosen, k, out))
            for chosen, k, out in found:
                out = out.astype(jnp.bfloat16)
                for i, f in enumerate(chosen):
                    mine[f, k] = out[2 * i * slab : (2 * i + 1) * slab]
                    theirs[f, k] = out[(2 * i + 1) * slab : (2 * i + 2) * slab]
            return 0

        lax.fori_loop(0, (bounds[q + 1] - bounds[q]) * fine // 16, one, 0)
        for f in which:
            keep_copy(f, q).start()
            back_copy(f, q).start()

    def met(f, part):
        twin_copy(f, part).wait_recv()

    def begin():
        edges_out()
        for load in table_loads:
            load.start()
        damp_load.wait()
        edges_in()
        for load in strip_loads(0):
            load.start()
        for n in range(4):
            prepare(n)

    def table_in():
        for load in table_loads:
            load.wait()

    P = functools.partial
    tasks = {
        0: [begin],
        1: [P(prepare, n) for n in range(4, strips)],
        2: [P(prepare, n) for n in range(strips, strips + 4)],
        4: [P(prepare, n) for n in range(strips + 4, 2 * strips)],
        3: [table_in],
    }
    for turn_of, f in enumerate(order):
        for n in range(slab // group):
            begin = early + turn_of * parts + n * group // planes
            end = begin + group // planes
            ready = end - (2 if turn_of == 2 else 1)
            tasks.setdefault(ready, []).append(P(azi_in, begin, end))
            tasks[ready].append(P(transform, f, n))
    more = {
        11: [P(give, 1), P(take, 1)],
        13: [P(met, 1, 0), P(met, 1, 1), P(solve, [1], 0)],
        14: [P(solve, [1], 1)],
        15: [P(solve, [1], 2)],
        19: [P(give, 2), P(take, 2)],
        21: [P(met, 2, 0), P(met, 2, 1), P(solve, [2], 0)],
        22: [P(solve, [2], 1), P(solve, [2], 2)],
        24: [P(solve, [1, 2], 3)],
        25: [P(solve, [1, 2], 4)],
        26: [P(give, 0), P(take, 0)],
        27: [P(solve, [1, 2], 5)],
        28: [P(met, 0, 0)]
        + [P(solve, [0], q) for q in range(4)]
        + [P(solve, [1, 2], 7), P(met, 0, 1)]
        + [P(solve, [0], q) for q in (4, 5, 7)],
        29: [P(solve, [0, 1, 2], 6)],
        30: [P(solve, [0, 1, 2], 8)],
    }
    for t, found in more.items():
        tasks.setdefault(t, []).extend(found)

    shard_load.wait()
    for t in range(ticks - 1):
        receive(t - lag)
        send(t)
        for task in tasks.get(t, []):
            task()

    edges_sent()
    for t in range(ticks - 1):
        sent(t)
    for f in range(fields):
        for part in range(2):
            if f != order[0]:
                twin_copy(f, part).wait_send()
        for q in range(blocks):
            keep_copy(f, q).wait()
            back_copy(f, q).wait()


def solved_modes(shard, table, cotangent, heat, tangent, wet):
    slab, radial, local = heat.shape
    half, rows, _ = shard.shape
    count = 2 * half
    strip = 16
    dma = pltpu.SemaphoreType.DMA
    out = jax.ShapeDtypeStruct((2 * count, slab, radial), jnp.bfloat16)
    modes = pltpu.VMEM((fields, count, slab, radial), jnp.bfloat16)
    return pl.pallas_call(
        modes_kernel,
        out_shape=[out] * fields,
        in_specs=[pl.BlockSpec(memory_space=pl.ANY)] * 6,
        out_specs=[pl.BlockSpec(memory_space=pl.ANY)] * fields,
        scratch_shapes=[
            pltpu.VMEM((radial // rows, count, rows, radial), jnp.bfloat16),
            pltpu.VMEM((2 * count, 2 * local), jnp.bfloat16),
            pltpu.VMEM((fields, slab * radial, 2 * local), jnp.bfloat16),
            pltpu.VMEM((2 * slab * count, radial), jnp.float32),
            modes,
            modes,
            pltpu.VMEM((2, count, slab, radial), jnp.bfloat16),
            pltpu.VMEM((2, 2, slab + 2, strip, local), jnp.float32),
            pltpu.VMEM((2, 2, radial, local), jnp.float32),
            pltpu.VMEM((slab, local), jnp.int32),
            dma((blocks, 4)), dma((blocks, 4)),
            dma((blocks + len(crossed), 3)), dma((blocks + len(crossed), 3)),
            dma((blocks + len(crossed), 3)), dma((blocks + len(crossed), 3)),
            dma((early + fields * parts,)), dma((early + fields * parts,)),
            dma((fields, 2)), dma((fields, 2)),
            dma((fields, blocks)), dma((fields, blocks)), dma((fields, blocks)),
            dma((2,)), dma((4, 2)), dma((2, 6)), dma((2, 2)), dma((2, 2)),
        ],
        compiler_params=pltpu.CompilerParams(
            collective_id=0, has_side_effects=True, vmem_limit_bytes=62 * 1024 * 1024
        ),
        cost_estimate=pl.CostEstimate(flops=15 * 10**9, bytes_accessed=10**8, transcendentals=0),
    )(shard, table, cotangent, heat, tangent, wet)


def edged_gradient_kernel(wet, heat, dual, before, after, out):
    rows = heat.shape[1]
    at = pl.ds(pl.multiple_of(pl.program_id(0) * rows, rows), rows)
    gradient_kernel(wet, heat, dual, before.at[:, at], after.at[:, at], out)


def edged_gradient(wet, heat, dual, before, after):
    slab, radial, lanes = heat.shape
    rows = 32
    spec = pl.BlockSpec((slab, rows, lanes), lambda i: (0, i, 0))
    whole = pl.BlockSpec(memory_space=pltpu.VMEM)
    return pl.pallas_call(
        edged_gradient_kernel,
        grid=(radial // rows,),
        in_specs=[whole, spec, spec, whole, whole],
        out_specs=spec,
        out_shape=jax.ShapeDtypeStruct(heat.shape, jnp.float32),
        cost_estimate=pl.CostEstimate(
            flops=10 * heat.size, bytes_accessed=10 * heat.size, transcendentals=heat.size
        ),
    )(wet, heat, dual, before, after)


def fused_body(table, heat_state, tangent_in, cotangent, wet_mask, sensors, propagators):
    slab, radial, local_azi = heat_state.shape
    depth = lax.axis_size("depth")
    me = lax.axis_index("azi")
    core = lax.rem(lax.axis_index("depth"), 2)
    modes = propagators.shape[0]
    half = modes // 2

    mine = lax.dynamic_slice_in_dim(propagators, core * half, half, axis=0)
    outgoing = lax.dynamic_slice_in_dim(propagators, (1 - core) * half, half, axis=0)
    incoming = lax.ppermute(outgoing, "depth", [(i, i ^ 1) for i in range(depth)])
    shard = jnp.concatenate(
        [jnp.where(core == 0, mine, incoming), jnp.where(core == 0, incoming, mine)], axis=1
    )

    def table_rows(which):
        return [
            lax.dynamic_slice_in_dim(table, owner * modes + which * half, half, axis=0)
            for owner in (me, 1 - me)
        ]

    own_rows = jnp.concatenate(table_rows(core), axis=0)
    twin_rows = jnp.concatenate(table_rows(1 - core), axis=0)

    def columns(weights, owner):
        return lax.dynamic_slice_in_dim(weights, owner * local_azi, local_azi, axis=1)

    to_azimuths = columns(jnp.concatenate([own_rows, twin_rows], axis=0), me)

    dual_modes, forward_modes, tangent_modes = solved_modes(
        shard, table, cotangent, heat_state, tangent_in, wet_mask
    )

    def inverse(solved):
        return jnp.einsum(
            "ka,kzr->zra", to_azimuths, solved, preferred_element_type=jnp.float32
        ).astype(jnp.bfloat16)

    dual = inverse(dual_modes)
    gradient = edged_gradient(wet_mask, heat_state, dual, *halo_planes(dual[-1:], dual[:1]))
    new_state = inverse(forward_modes)
    radial_index = jnp.arange(radial, dtype=jnp.int32)[None, :, None]
    selected = jnp.where(radial_index == sensors[:, None, :], new_state, jnp.zeros_like(new_state))
    readings = jnp.sum(selected, axis=1)
    tangent_out = inverse(tangent_modes)
    return (new_state, tangent_out, gradient, readings)


def solution(mesh):
    def run(heat_state, tangent_in, cotangent, wet_mask, sensors, propagators):
        table = jnp.asarray(fourier_table(heat_state.shape[2]))
        field = P("depth", None, "azi")
        fits = mesh.shape["azi"] == 2 and mesh.shape["depth"] == 16
        body = fused_body if fits else split_body
        panel = P("depth", "azi")
        return jax.shard_map(
            body,
            mesh=mesh,
            in_specs=(P(), field, field, field, panel, panel, P("azi", "depth", None)),
            out_specs=(field, field, field, panel),
            check_vma=False,
        )(table, heat_state, tangent_in, cotangent, wet_mask, sensors, propagators)

    return run
```

```python
import functools
import math

import jax
import jax.numpy as jnp
import numpy as np
from jax import lax
from jax.experimental import pallas as pl
from jax.experimental.pallas import tpu as pltpu
from jax.sharding import PartitionSpec as P

mixing = 0.25
evaporation = 0.6
skin_depth = 16.0
mode_chunks = 2


def halo_planes(last, first):
    size = lax.axis_size("depth")
    up = [(i, i + 1) for i in range(size - 1)]
    down = [(j, i) for i, j in up]
    before = lax.ppermute(last, "depth", up)
    after = lax.ppermute(first, "depth", down)
    return before, after


def damping_profile(rows, lanes):
    radius = pl.program_id(0) * rows + lax.broadcasted_iota(jnp.int32, (rows, lanes), 0)
    return evaporation * jnp.exp(-radius.astype(jnp.float32) / skin_depth)


def plane(ref, before, after, z):
    source, index = (before, 0) if z < 0 else (after, 0) if z == ref.shape[0] else (ref, z)
    return source[index].astype(jnp.float32)


def mixed(ref, before, after, z):
    centre = plane(ref, before, after, z)
    around = plane(ref, before, after, z + 1) + plane(ref, before, after, z - 1)
    return centre, centre + mixing * (around - 2.0 * centre)


def rhs_kernel(wet, heat, heat_before, heat_after, tangent, tangent_before, tangent_after, out, tangent_out):
    slab, rows, lanes = heat.shape
    profile = damping_profile(rows, lanes)
    for z in range(slab):
        damping = wet[z : z + 1].astype(jnp.float32) * profile
        centre, value = mixed(heat, heat_before, heat_after, z)
        moisture = jnp.tanh(centre)
        out[z] = (value - damping * moisture).astype(out.dtype)
        slope = 1.0 - moisture * moisture
        centre, value = mixed(tangent, tangent_before, tangent_after, z)
        tangent_out[z] = (value - damping * slope * centre).astype(tangent_out.dtype)


def gradient_kernel(wet, heat, dual, dual_before, dual_after, out):
    slab, rows, lanes = heat.shape
    profile = damping_profile(rows, lanes)
    for z in range(slab):
        damping = wet[z : z + 1].astype(jnp.float32) * profile
        moisture = jnp.tanh(heat[z])
        slope = 1.0 - moisture * moisture
        centre, value = mixed(dual, dual_before, dual_after, z)
        out[z] = value - damping * slope * centre


def by_radius(kernel, wet, fields, dtypes):
    slab, radial, lanes = fields[0].shape
    rows = min(radial, 16)

    def spec(depth):
        return pl.BlockSpec((depth, rows, lanes), lambda i: (0, i, 0))

    count = len(dtypes) * slab * radial * lanes
    return pl.pallas_call(
        kernel,
        grid=(radial // rows,),
        in_specs=[pl.BlockSpec(wet.shape, lambda i: (0, 0))] + [spec(f.shape[0]) for f in fields],
        out_specs=[spec(slab) for _ in dtypes],
        out_shape=[jax.ShapeDtypeStruct((slab, radial, lanes), dtype) for dtype in dtypes],
        cost_estimate=pl.CostEstimate(flops=10 * count, bytes_accessed=6 * count, transcendentals=count),
    )(wet, *fields)


def fourier_table(length):
    wavenumber = np.arange(length, dtype=np.int32)[:, None]
    position = np.arange(length, dtype=np.int32)[None, :]
    midpoint = length // 2
    harmonic = np.where(wavenumber <= midpoint, wavenumber, wavenumber - midpoint)
    phase = (harmonic * position % length).astype(np.float32) * np.float32(2.0 * math.pi / length)
    waveform = np.where(wavenumber <= midpoint, np.cos(phase), np.sin(phase))
    boundary = (wavenumber == 0) | (wavenumber == midpoint)
    weights = np.where(boundary, math.sqrt(1.0 / length), math.sqrt(2.0 / length)).astype(np.float32)
    return (waveform * weights).astype(jnp.bfloat16)


def from_all(value):
    size = lax.axis_size("azi")
    blocks = [value]
    for shift in range(1, size):
        pairs = [(i, (i + shift) % size) for i in range(size)]
        blocks.append(lax.ppermute(value, "azi", pairs))
    return blocks


def split_body(table, heat_state, tangent_in, cotangent, wet_mask, sensors, propagators):
    slab, radial, local_azi = heat_state.shape
    size = lax.axis_size("azi")
    me = lax.axis_index("azi")
    owners = [lax.rem(me - shift + size, size) for shift in range(size)]
    modes = propagators.shape[0]
    step = modes // mode_chunks

    whole = [
        lax.all_gather(propagators[c * step : (c + 1) * step], "depth", axis=1, tiled=True)
        for c in range(mode_chunks)
    ]

    own_modes = lax.dynamic_slice_in_dim(table, me * modes, modes, axis=0)
    to_modes = [
        lax.dynamic_slice_in_dim(own_modes, owner * local_azi, local_azi, axis=1) for owner in owners
    ]
    own_azimuths = lax.dynamic_slice_in_dim(table, me * local_azi, local_azi, axis=1)
    to_azimuths = [
        lax.dynamic_slice_in_dim(own_azimuths, owner * modes, modes, axis=0) for owner in owners
    ]

    def part_spectrum(weights, block, c):
        return jnp.einsum(
            "ka,zra->kzr",
            weights[c * step : (c + 1) * step],
            block,
            preferred_element_type=jnp.float32,
        )

    seed_blocks = from_all(cotangent.astype(jnp.bfloat16))
    seed_part, heat_last, heat_first, tangent_last, tangent_first = lax.optimization_barrier(
        (
            part_spectrum(to_modes[0], seed_blocks[0], 0),
            heat_state[-1:],
            heat_state[:1],
            tangent_in[-1:],
            tangent_in[:1],
        )
    )

    forward_rhs, tangent_rhs = by_radius(
        rhs_kernel,
        wet_mask,
        [heat_state, *halo_planes(heat_last, heat_first), tangent_in, *halo_planes(tangent_last, tangent_first)],
        [jnp.bfloat16] * 2,
    )
    own_seed, forward_rhs, tangent_rhs = lax.optimization_barrier(
        (seed_blocks[0], forward_rhs, tangent_rhs)
    )
    seed_blocks = [own_seed] + seed_blocks[1:]
    forward_blocks = from_all(forward_rhs)
    tangent_blocks = from_all(tangent_rhs)

    def solve(blocks, formula, first=None):
        returned = []
        for c in range(mode_chunks):
            known = c == 0 and first is not None
            total = first if known else part_spectrum(to_modes[0], blocks[0], c)
            for weights, block in zip(to_modes[1:], blocks[1:]):
                total = total + part_spectrum(weights, block, c)
            solved = jnp.einsum(
                formula, whole[c], total.astype(jnp.bfloat16), preferred_element_type=jnp.float32
            ).astype(jnp.bfloat16)
            returned.append(from_all(solved))
        return returned

    def part_inverse(returned, pairs):
        total = 0.0
        for c, i in pairs:
            total = total + jnp.einsum(
                "ka,kzr->zra",
                to_azimuths[i][c * step : (c + 1) * step],
                returned[c][i],
                preferred_element_type=jnp.float32,
            )
        return total

    pairs = [(c, i) for i in range(size) for c in range(mode_chunks)]

    def inverse(returned):
        return part_inverse(returned, pairs).astype(jnp.bfloat16)

    dual_modes = solve(seed_blocks, "ksr,kzs->kzr", seed_part)
    dual_modes[0][0], *forward_received = lax.optimization_barrier(
        (dual_modes[0][0], *forward_blocks[1:])
    )
    forward_blocks = forward_blocks[:1] + forward_received
    forward_modes = solve(forward_blocks, "krs,kzs->kzr")
    tangent_modes = solve(tangent_blocks, "krs,kzs->kzr")

    dual = inverse(dual_modes)
    (gradient,) = by_radius(
        gradient_kernel, wet_mask, [heat_state, dual, *halo_planes(dual[-1:], dual[:1])], [jnp.float32]
    )

    new_state = inverse(forward_modes)
    radial_index = jnp.arange(radial, dtype=jnp.int32)[None, :, None]
    selected = jnp.where(radial_index == sensors[:, None, :], new_state, jnp.zeros_like(new_state))
    readings = jnp.sum(selected, axis=1)

    partial = part_inverse(tangent_modes, pairs[:-1])
    gradient, partial, tangent_modes[-1][-1] = lax.optimization_barrier(
        (gradient, partial, tangent_modes[-1][-1])
    )
    tangent_out = (partial + part_inverse(tangent_modes, pairs[-1:])).astype(jnp.bfloat16)
    return (new_state, tangent_out, gradient, readings)


fields = 3
parts = 8
early = parts // 2
bounds = (0, 2, 4, 6, 8, 10, 12, 13, 15, 16)
blocks = len(bounds) - 1
sections = ((0, 1, 2), (3, 4, 5), (6, 7, 8))
crossed = (7, 8)
order = (1, 2, 0)
own, other = 0, 1
ticks = 32


def timed(items):
    found = [[] for _ in range(ticks)]
    start = 0
    for item in items:
        found[start // 2].append(item)
        start += bounds[item[0] + 1] - bounds[item[0]]
    return found


def line_order():
    found = []
    for section in sections:
        group = [(q, c) for q in section for c in ((own, other) if q in crossed else (own,))]
        found += [(q, c, p) for p in range(3) for q, c in group]
    return timed(found)


def pair_order():
    found = []
    for section in sections:
        found += [(q, s) for s in range(4) for q in section if q not in crossed]
    found[10:10] = [(q, 0) for q in crossed]
    return timed(found)


def modes_kernel(
    shard, full, cotangent, heat, tangent, wet,
    out_seed, out_forward, out_tangent,
    matrices, table, values, stage, mine, theirs, given, raw, edges, edge_out, edge_in, damp,
    pair_send, pair_recv, up_send, up_recv, down_send, down_recv, azi_send, azi_recv,
    twin_send, twin_recv, back_send, back_recv, keep_sem, load_sem, table_sem, raw_sem, edge_load, edge_send, edge_recv,
):
    outs = (out_seed, out_forward, out_tangent)
    flips = (True, False, False)
    place, azi = lax.axis_index("depth"), lax.axis_index("azi")
    z, x, core = place // 4, place // 2 % 2, place % 2
    pair, twin, up, down = place + 2 - 4 * x, place + 1 - 2 * core, place + 4, place - 4
    count, radial = matrices.shape[1], matrices.shape[3]
    step = count // parts
    fine = count // bounds[-1]
    half = count // 2
    chips = matrices.shape[0]
    slab = mine.shape[2]
    local = heat.shape[2]
    strip = raw.shape[3]
    strips = radial // strip
    last = lax.axis_size("depth") - 1
    planes = slab // parts
    mesh_ids = pl.DeviceIdType.MESH

    barrier = pltpu.get_barrier_semaphore()

    def greet(where, azimuth):
        pl.semaphore_signal(barrier, inc=1, device_id=(where, azimuth), device_id_type=mesh_ids)

    greet(pair, azi)
    greet(twin, azi)
    greet(place, 1 - azi)

    @pl.when(z < 3)
    def _():
        greet(up, azi)

    @pl.when(z > 0)
    def _():
        greet(down, azi)

    @pl.when(place < last)
    def _():
        greet(place + 1, azi)

    @pl.when(place > 0)
    def _():
        greet(place - 1, azi)

    inner = (place + last) // (last + 1) + (2 * last - place) // (last + 1)
    pl.semaphore_wait(barrier, 4 + (z + 1) // 2 % 2 + inner)

    def remote(src, dst, send, recv, where, azimuth=azi):
        return pltpu.make_async_remote_copy(
            src_ref=src, dst_ref=dst, send_sem=send, recv_sem=recv,
            device_id=(where, azimuth), device_id_type=mesh_ids,
        )

    def span_of(q):
        return pl.ds(bounds[q] * fine, (bounds[q + 1] - bounds[q]) * fine)

    def region(q, line, side):
        return matrices.at[2 * line + side, span_of(q)]

    flipped = (z, z + 1 - 2 * (z % 2), z + 2 - 4 * (z // 2), 3 - z)

    def pair_copy(q, s):
        ref = region(q, flipped[s], x)
        return remote(ref, ref, pair_send.at[q, s], pair_recv.at[q, s], pair)

    def line_item(q, c):
        return blocks + crossed.index(q) if c == other else q

    def up_copy(q, c, p):
        ref = region(q, z - p, x if c == own else 1 - x)
        k = line_item(q, c)
        return remote(ref, ref, up_send.at[k, p], up_recv.at[k, p], up)

    def down_copy(q, c, p):
        ref = region(q, z + p, x if c == own else 1 - x)
        k = line_item(q, c)
        return remote(ref, ref, down_send.at[k, p], down_recv.at[k, p], down)

    def azi_copy(n):
        if n < early:
            mine_at = matrices.at[2 * z + x, pl.ds(n * step, step)]
            theirs_at = matrices.at[2 * z + x, pl.ds(half + n * step, step)]
            return remote(mine_at, theirs_at, azi_send.at[n], azi_recv.at[n], place, 1 - azi)
        turn_of, part = divmod(n - early, parts)
        f = order[turn_of]
        span = planes * radial
        at = pl.ds(part * span, span)
        return remote(
            values.at[f, at, pl.ds(0, local)],
            values.at[f, at, pl.ds(local, local)],
            azi_send.at[n], azi_recv.at[n], place, 1 - azi,
        )

    pairs, lines, azis = pair_order(), line_order(), early + fields * parts

    lag, lead = 2, 4

    def each(t, act):
        if 0 <= t < ticks:
            for item in pairs[t]:
                act(pair_copy(*item))

    def azi_until(t):
        return early if t < 2 else min(t + lead + 1, azis)

    def azi_send_up_to(t):
        for n in range(0 if t == 0 else azi_until(t - 1), azi_until(t)):
            azi_copy(n).start()

    def azi_in(begin, end):
        for n in range(begin, end):
            azi_copy(n).wait_recv()

    def send(t):
        each(t, lambda copy: copy.start())
        azi_send_up_to(t)
        for q, c, p in lines[t] if t < ticks else ():

            @pl.when((z < 3) & (z >= p))
            def _():
                up_copy(q, c, p).start()

            @pl.when((z > 0) & (z + p <= 3))
            def _():
                down_copy(q, c, p).start()

    def receive(t):
        if t == early:
            azi_in(0, early)
        each(t, lambda copy: copy.wait_recv())
        for q, c, p in lines[t] if 0 <= t < ticks else ():

            @pl.when(z >= p + 1)
            def _():
                up_copy(q, c, p).wait_recv()

            @pl.when(z + p + 1 <= 3)
            def _():
                down_copy(q, c, p).wait_recv()

    def sent(t):
        each(t, lambda copy: copy.wait_send())
        if t < azis:
            azi_copy(t).wait_send()
        for q, c, p in lines[t]:

            @pl.when((z < 3) & (z >= p))
            def _():
                up_copy(q, c, p).wait_send()

            @pl.when((z > 0) & (z + p <= 3))
            def _():
                down_copy(q, c, p).wait_send()

    shard_load = pltpu.make_async_copy(
        shard, matrices.at[2 * z + x, pl.ds(0, half)], load_sem.at[0]
    )
    shard_load.start()
    damp_load = pltpu.make_async_copy(wet, damp, load_sem.at[1])
    damp_load.start()

    def strip_loads(n):
        slot = n % 2
        c = n % strips
        span = pl.ds(c * strip, strip)
        if n >= strips:
            return [
                pltpu.make_async_copy(
                    cotangent.at[:, span, :], raw.at[slot, 0, pl.ds(1, slab)], raw_sem.at[slot, 0]
                )
            ]
        found = []
        for f, source in enumerate((heat, tangent)):
            found.append((source.at[:, span, :], raw.at[slot, f, pl.ds(1, slab)], 3 * f))
            found.append((edges.at[f, 0, span], raw.at[slot, f, 0], 3 * f + 1))
            found.append((edges.at[f, 1, span], raw.at[slot, f, slab + 1], 3 * f + 2))
        return [pltpu.make_async_copy(a, b, raw_sem.at[slot, i]) for a, b, i in found]

    def edge_copies(side):
        out = []
        for f in range(2):
            out.append(
                remote(
                    edge_out.at[f, side], edge_in.at[f, side],
                    edge_send.at[f, side], edge_recv.at[f, side],
                    place + 1 if side == 0 else place - 1,
                )
            )
        return out

    edge_loads = [
        pltpu.make_async_copy(
            source.at[slab - 1 if side == 0 else 0], edges.at[f, side], edge_load.at[f, side]
        )
        for f, source in enumerate((heat, tangent))
        for side in range(2)
    ]

    def edges_out():
        for load in edge_loads:
            load.start()
        for load in edge_loads:
            load.wait()
        edge_out[...] = edges[...].astype(jnp.bfloat16)

        @pl.when(place < last)
        def _():
            for copy in edge_copies(0):
                copy.start()

        @pl.when(place > 0)
        def _():
            for copy in edge_copies(1):
                copy.start()

    def edges_in():
        for side, empty, full_side in ((0, place == 0, place > 0), (1, place == last, place < last)):

            @pl.when(full_side)
            def _():
                for copy in edge_copies(side):
                    copy.wait_recv()
                edges[:, side] = edge_in[:, side].astype(jnp.float32)

            @pl.when(empty)
            def _():
                edges[:, side] = jnp.zeros((2, radial, local), jnp.float32)

    def edges_sent():
        @pl.when(place < last)
        def _():
            for copy in edge_copies(0):
                copy.wait_send()

        @pl.when(place > 0)
        def _():
            for copy in edge_copies(1):
                copy.wait_send()

    table_loads = []
    for part in range(4):
        owner, which = (azi, 1 - azi)[part % 2], (1 - core, core)[part // 2]
        row = pl.multiple_of((2 * owner + which) * (half), half)
        for h in range(2):
            col = pl.multiple_of((azi, 1 - azi)[h] * local, local)
            table_loads.append(
                pltpu.make_async_copy(
                    full.at[pl.ds(row, half), pl.ds(col, local)],
                    table.at[pl.ds(part * half, half), pl.ds(h * local, local)],
                    table_sem.at[part, h],
                )
            )

    def prepare(n):
        slot = n % 2
        c = n % strips
        if n + 1 < 2 * strips:
            for load in strip_loads(n + 1):
                load.start()
        for load in strip_loads(n):
            load.wait()
        radius = c * strip + lax.broadcasted_iota(jnp.int32, (strip, local), 0)
        profile = evaporation * jnp.exp(-radius.astype(jnp.float32) / skin_depth)

        def plane_step(p, _):
            into = pl.ds(pl.multiple_of(p * radial + c * strip, strip), strip)
            if n >= strips:
                values[0, into, pl.ds(0, local)] = raw[slot, 0, p + 1].astype(jnp.bfloat16)
                return 0
            damping = damp[pl.ds(p, 1), :].astype(jnp.float32) * profile

            def mix(f):
                centre = raw[slot, f, p + 1]
                around = raw[slot, f, p + 2] + raw[slot, f, p]
                return centre, centre + mixing * (around - 2.0 * centre)

            centre, value = mix(0)
            moisture = jnp.tanh(centre)
            values[1, into, pl.ds(0, local)] = (value - damping * moisture).astype(jnp.bfloat16)
            slope = 1.0 - moisture * moisture
            centre, value = mix(1)
            values[2, into, pl.ds(0, local)] = (value - damping * slope * centre).astype(jnp.bfloat16)
            return 0

        lax.fori_loop(0, slab, plane_step, 0)

    def twin_copy(f, part):
        at = pl.ds(part * half, half)
        return remote(
            given.at[order.index(f) % 2, at], theirs.at[f, at], twin_send.at[f, part], twin_recv.at[f, part], twin
        )

    group = 4

    def transform(f, n):
        span = group * radial
        cols = values[f, pl.ds(n * span, span), :]

        def half_step(h, _):
            weights = table[pl.ds(pl.multiple_of(h * count, count), count), :]
            out = lax.dot_general(
                weights, cols, (((1,), (1,)), ((), ())), preferred_element_type=jnp.float32
            )
            for g in range(group):
                at = pl.multiple_of((n * group + g) * 2 * count + h * count, count)
                stage[pl.ds(at, count), :] = out[:, g * radial : (g + 1) * radial]
            return 0

        lax.fori_loop(0, 2, half_step, 0)

    def turn(into, f, first, begin, end):
        def one(n, _):
            for u in range(8):
                k = n * 8 + u
                into[f, k] = stage[pl.ds(first + k, slab, stride=2 * count), :].astype(jnp.bfloat16)
            return 0

        lax.fori_loop(begin // 8, end // 8, one, 0)

    def give(f):
        for part in range(2):
            if f == order[2]:
                twin_copy(order[0], part).wait_send()
            turn(given, order.index(f) % 2, 0, part * half, (part + 1) * half)
            twin_copy(f, part).start()

    def take(f):
        turn(mine, f, count, 0, count)

    def keep_copy(f, q):
        at = span_of(q)
        return pltpu.make_async_copy(mine.at[f, at], outs[f].at[at], keep_sem.at[f, q])

    def back_copy(f, q):
        return remote(
            theirs.at[f, span_of(q)],
            outs[f].at[pl.ds(count + bounds[q] * fine, (bounds[q + 1] - bounds[q]) * fine)],
            back_send.at[f, q], back_recv.at[f, q], twin,
        )

    def solve(which, q):
        def one(n, _):
            found = []
            for u in range(16):
                k = bounds[q] * fine + n * 16 + u
                matrix = jnp.concatenate([matrices[c, k] for c in range(chips)], axis=0)
                for flip in (True, False):
                    chosen = [f for f in which if flips[f] == flip]
                    if not chosen:
                        continue
                    stacked = jnp.concatenate(
                        [part[f, k] for f in chosen for part in (mine, theirs)], axis=0
                    )
                    out = lax.dot_general(
                        stacked, matrix, (((1,), (0 if flip else 1,)), ((), ())),
                        preferred_element_type=jnp.float32,
                    )
                    found.append((chosen, k, out))
            for chosen, k, out in found:
                out = out.astype(jnp.bfloat16)
                for i, f in enumerate(chosen):
                    mine[f, k] = out[2 * i * slab : (2 * i + 1) * slab]
                    theirs[f, k] = out[(2 * i + 1) * slab : (2 * i + 2) * slab]
            return 0

        lax.fori_loop(0, (bounds[q + 1] - bounds[q]) * fine // 16, one, 0)
        for f in which:
            keep_copy(f, q).start()
            back_copy(f, q).start()

    def met(f, part):
        twin_copy(f, part).wait_recv()

    def begin():
        edges_out()
        for load in table_loads:
            load.start()
        damp_load.wait()
        edges_in()
        for load in strip_loads(0):
            load.start()
        for n in range(4):
            prepare(n)

    def table_in():
        for load in table_loads:
            load.wait()

    P = functools.partial
    tasks = {
        0: [begin],
        1: [P(prepare, n) for n in range(4, strips)],
        2: [P(prepare, n) for n in range(strips, strips + 4)],
        4: [P(prepare, n) for n in range(strips + 4, 2 * strips)],
        3: [table_in],
    }
    for turn_of, f in enumerate(order):
        for n in range(slab // group):
            begin = early + turn_of * parts + n * group // planes
            end = begin + group // planes
            ready = end - (2 if turn_of == 2 else 1)
            tasks.setdefault(ready, []).append(P(azi_in, begin, end))
            tasks[ready].append(P(transform, f, n))
    more = {
        11: [P(give, 1), P(take, 1)],
        13: [P(met, 1, 0), P(met, 1, 1), P(solve, [1], 0)],
        14: [P(solve, [1], 1)],
        15: [P(solve, [1], 2)],
        19: [P(give, 2), P(take, 2)],
        21: [P(met, 2, 0), P(met, 2, 1), P(solve, [2], 0)],
        22: [P(solve, [2], 1), P(solve, [2], 2)],
        24: [P(solve, [1, 2], 3)],
        25: [P(solve, [1, 2], 4)],
        26: [P(give, 0), P(take, 0), P(solve, [1, 2], 5)],
        27: [P(met, 0, 0)] + [P(solve, [0], q) for q in range(4)],
        28: [P(solve, [1, 2], 7), P(met, 0, 1)] + [P(solve, [0], q) for q in (4, 5, 7)],
        29: [P(solve, [0, 1, 2], 6)],
        30: [P(solve, [0, 1, 2], 8)],
    }
    for t, found in more.items():
        tasks.setdefault(t, []).extend(found)

    shard_load.wait()
    for t in range(ticks - 1):
        receive(t - lag)
        send(t)
        for task in tasks.get(t, []):
            task()

    edges_sent()
    for t in range(ticks - 1):
        sent(t)
    for f in range(fields):
        for part in range(2):
            if f != order[0]:
                twin_copy(f, part).wait_send()
        for q in range(blocks):
            keep_copy(f, q).wait()
            back_copy(f, q).wait()


def solved_modes(shard, table, cotangent, heat, tangent, wet):
    slab, radial, local = heat.shape
    half, rows, _ = shard.shape
    count = 2 * half
    strip = 16
    dma = pltpu.SemaphoreType.DMA
    out = jax.ShapeDtypeStruct((2 * count, slab, radial), jnp.bfloat16)
    modes = pltpu.VMEM((fields, count, slab, radial), jnp.bfloat16)
    return pl.pallas_call(
        modes_kernel,
        out_shape=[out] * fields,
        in_specs=[pl.BlockSpec(memory_space=pl.ANY)] * 6,
        out_specs=[pl.BlockSpec(memory_space=pl.ANY)] * fields,
        scratch_shapes=[
            pltpu.VMEM((radial // rows, count, rows, radial), jnp.bfloat16),
            pltpu.VMEM((2 * count, 2 * local), jnp.bfloat16),
            pltpu.VMEM((fields, slab * radial, 2 * local), jnp.bfloat16),
            pltpu.VMEM((2 * slab * count, radial), jnp.float32),
            modes,
            modes,
            pltpu.VMEM((2, count, slab, radial), jnp.bfloat16),
            pltpu.VMEM((2, 2, slab + 2, strip, local), jnp.float32),
            pltpu.VMEM((2, 2, radial, local), jnp.float32),
            pltpu.VMEM((2, 2, radial, local), jnp.bfloat16),
            pltpu.VMEM((2, 2, radial, local), jnp.bfloat16),
            pltpu.VMEM((slab, local), jnp.int32),
            dma((blocks, 4)), dma((blocks, 4)),
            dma((blocks + len(crossed), 3)), dma((blocks + len(crossed), 3)),
            dma((blocks + len(crossed), 3)), dma((blocks + len(crossed), 3)),
            dma((early + fields * parts,)), dma((early + fields * parts,)),
            dma((fields, 2)), dma((fields, 2)),
            dma((fields, blocks)), dma((fields, blocks)), dma((fields, blocks)),
            dma((2,)), dma((4, 2)), dma((2, 6)), dma((2, 2)), dma((2, 2)), dma((2, 2)),
        ],
        compiler_params=pltpu.CompilerParams(
            collective_id=0, has_side_effects=True, vmem_limit_bytes=62 * 1024 * 1024
        ),
        cost_estimate=pl.CostEstimate(flops=15 * 10**9, bytes_accessed=10**8, transcendentals=0),
    )(shard, table, cotangent, heat, tangent, wet)


def edged_gradient_kernel(wet, heat, dual, before, after, out):
    rows = heat.shape[1]
    at = pl.ds(pl.multiple_of(pl.program_id(0) * rows, rows), rows)
    gradient_kernel(wet, heat, dual, before.at[:, at], after.at[:, at], out)


def edged_gradient(wet, heat, dual, before, after):
    slab, radial, lanes = heat.shape
    rows = 32
    spec = pl.BlockSpec((slab, rows, lanes), lambda i: (0, i, 0))
    whole = pl.BlockSpec(memory_space=pltpu.VMEM)
    return pl.pallas_call(
        edged_gradient_kernel,
        grid=(radial // rows,),
        in_specs=[whole, spec, spec, whole, whole],
        out_specs=spec,
        out_shape=jax.ShapeDtypeStruct(heat.shape, jnp.float32),
        cost_estimate=pl.CostEstimate(
            flops=10 * heat.size, bytes_accessed=10 * heat.size, transcendentals=heat.size
        ),
    )(wet, heat, dual, before, after)


def fused_body(table, heat_state, tangent_in, cotangent, wet_mask, sensors, propagators):
    slab, radial, local_azi = heat_state.shape
    depth = lax.axis_size("depth")
    me = lax.axis_index("azi")
    core = lax.rem(lax.axis_index("depth"), 2)
    modes = propagators.shape[0]
    half = modes // 2

    mine = lax.dynamic_slice_in_dim(propagators, core * half, half, axis=0)
    outgoing = lax.dynamic_slice_in_dim(propagators, (1 - core) * half, half, axis=0)
    incoming = lax.ppermute(outgoing, "depth", [(i, i ^ 1) for i in range(depth)])
    rows = mine.shape[1]
    at_core = lax.broadcasted_iota(jnp.int32, (1, 2, 1, 1), 1) == core
    shard = jnp.where(at_core, mine[:, None], incoming[:, None]).reshape(half, 2 * rows, radial)

    def table_rows(which):
        return [
            lax.dynamic_slice_in_dim(table, owner * modes + which * half, half, axis=0)
            for owner in (me, 1 - me)
        ]

    own_rows = jnp.concatenate(table_rows(core), axis=0)
    twin_rows = jnp.concatenate(table_rows(1 - core), axis=0)

    def columns(weights, owner):
        return lax.dynamic_slice_in_dim(weights, owner * local_azi, local_azi, axis=1)

    to_azimuths = columns(jnp.concatenate([own_rows, twin_rows], axis=0), me)

    dual_modes, forward_modes, tangent_modes = solved_modes(
        shard, table, cotangent, heat_state, tangent_in, wet_mask
    )

    def inverse(solved):
        return jnp.einsum(
            "ka,kzr->zra", to_azimuths, solved, preferred_element_type=jnp.float32
        ).astype(jnp.bfloat16)

    dual = inverse(dual_modes)
    gradient = edged_gradient(wet_mask, heat_state, dual, *halo_planes(dual[-1:], dual[:1]))
    new_state = inverse(forward_modes)
    radial_index = jnp.arange(radial, dtype=jnp.int32)[None, :, None]
    selected = jnp.where(radial_index == sensors[:, None, :], new_state, jnp.zeros_like(new_state))
    readings = jnp.sum(selected, axis=1)
    tangent_out = inverse(tangent_modes)
    return (new_state, tangent_out, gradient, readings)


def solution(mesh):
    def run(heat_state, tangent_in, cotangent, wet_mask, sensors, propagators):
        table = jnp.asarray(fourier_table(heat_state.shape[2]))
        field = P("depth", None, "azi")
        fits = mesh.shape["azi"] == 2 and mesh.shape["depth"] == 16
        body = fused_body if fits else split_body
        panel = P("depth", "azi")
        return jax.shard_map(
            body,
            mesh=mesh,
            in_specs=(P(), field, field, field, panel, panel, P("azi", "depth", None)),
            out_specs=(field, field, field, panel),
            check_vma=False,
        )(table, heat_state, tangent_in, cotangent, wet_mask, sensors, propagators)

    return run
```

```python
import functools
import math

import jax
import jax.numpy as jnp
import numpy as np
from jax import lax
from jax.experimental import pallas as pl
from jax.experimental.pallas import tpu as pltpu
from jax.sharding import PartitionSpec as P

mixing = 0.25
evaporation = 0.6
skin_depth = 16.0
mode_chunks = 2


def halo_planes(last, first):
    size = lax.axis_size("depth")
    up = [(i, i + 1) for i in range(size - 1)]
    down = [(j, i) for i, j in up]
    before = lax.ppermute(last, "depth", up)
    after = lax.ppermute(first, "depth", down)
    return before, after


def damping_profile(rows, lanes):
    radius = pl.program_id(0) * rows + lax.broadcasted_iota(jnp.int32, (rows, lanes), 0)
    return evaporation * jnp.exp(-radius.astype(jnp.float32) / skin_depth)


def plane(ref, before, after, z):
    source, index = (before, 0) if z < 0 else (after, 0) if z == ref.shape[0] else (ref, z)
    return source[index].astype(jnp.float32)


def mixed(ref, before, after, z):
    centre = plane(ref, before, after, z)
    around = plane(ref, before, after, z + 1) + plane(ref, before, after, z - 1)
    return centre, centre + mixing * (around - 2.0 * centre)


def rhs_kernel(wet, heat, heat_before, heat_after, tangent, tangent_before, tangent_after, out, tangent_out):
    slab, rows, lanes = heat.shape
    profile = damping_profile(rows, lanes)
    for z in range(slab):
        damping = wet[z : z + 1].astype(jnp.float32) * profile
        centre, value = mixed(heat, heat_before, heat_after, z)
        moisture = jnp.tanh(centre)
        out[z] = (value - damping * moisture).astype(out.dtype)
        slope = 1.0 - moisture * moisture
        centre, value = mixed(tangent, tangent_before, tangent_after, z)
        tangent_out[z] = (value - damping * slope * centre).astype(tangent_out.dtype)


def gradient_kernel(wet, heat, dual, dual_before, dual_after, out):
    slab, rows, lanes = heat.shape
    profile = damping_profile(rows, lanes)
    for z in range(slab):
        damping = wet[z : z + 1].astype(jnp.float32) * profile
        moisture = jnp.tanh(heat[z])
        slope = 1.0 - moisture * moisture
        centre, value = mixed(dual, dual_before, dual_after, z)
        out[z] = value - damping * slope * centre


def by_radius(kernel, wet, fields, dtypes):
    slab, radial, lanes = fields[0].shape
    rows = min(radial, 16)

    def spec(depth):
        return pl.BlockSpec((depth, rows, lanes), lambda i: (0, i, 0))

    count = len(dtypes) * slab * radial * lanes
    return pl.pallas_call(
        kernel,
        grid=(radial // rows,),
        in_specs=[pl.BlockSpec(wet.shape, lambda i: (0, 0))] + [spec(f.shape[0]) for f in fields],
        out_specs=[spec(slab) for _ in dtypes],
        out_shape=[jax.ShapeDtypeStruct((slab, radial, lanes), dtype) for dtype in dtypes],
        cost_estimate=pl.CostEstimate(flops=10 * count, bytes_accessed=6 * count, transcendentals=count),
    )(wet, *fields)


def fourier_table(length):
    wavenumber = np.arange(length, dtype=np.int32)[:, None]
    position = np.arange(length, dtype=np.int32)[None, :]
    midpoint = length // 2
    harmonic = np.where(wavenumber <= midpoint, wavenumber, wavenumber - midpoint)
    phase = (harmonic * position % length).astype(np.float32) * np.float32(2.0 * math.pi / length)
    waveform = np.where(wavenumber <= midpoint, np.cos(phase), np.sin(phase))
    boundary = (wavenumber == 0) | (wavenumber == midpoint)
    weights = np.where(boundary, math.sqrt(1.0 / length), math.sqrt(2.0 / length)).astype(np.float32)
    return (waveform * weights).astype(jnp.bfloat16)


def from_all(value):
    size = lax.axis_size("azi")
    blocks = [value]
    for shift in range(1, size):
        pairs = [(i, (i + shift) % size) for i in range(size)]
        blocks.append(lax.ppermute(value, "azi", pairs))
    return blocks


def split_body(table, heat_state, tangent_in, cotangent, wet_mask, sensors, propagators):
    slab, radial, local_azi = heat_state.shape
    size = lax.axis_size("azi")
    me = lax.axis_index("azi")
    owners = [lax.rem(me - shift + size, size) for shift in range(size)]
    modes = propagators.shape[0]
    step = modes // mode_chunks

    whole = [
        lax.all_gather(propagators[c * step : (c + 1) * step], "depth", axis=1, tiled=True)
        for c in range(mode_chunks)
    ]

    own_modes = lax.dynamic_slice_in_dim(table, me * modes, modes, axis=0)
    to_modes = [
        lax.dynamic_slice_in_dim(own_modes, owner * local_azi, local_azi, axis=1) for owner in owners
    ]
    own_azimuths = lax.dynamic_slice_in_dim(table, me * local_azi, local_azi, axis=1)
    to_azimuths = [
        lax.dynamic_slice_in_dim(own_azimuths, owner * modes, modes, axis=0) for owner in owners
    ]

    def part_spectrum(weights, block, c):
        return jnp.einsum(
            "ka,zra->kzr",
            weights[c * step : (c + 1) * step],
            block,
            preferred_element_type=jnp.float32,
        )

    seed_blocks = from_all(cotangent.astype(jnp.bfloat16))
    seed_part, heat_last, heat_first, tangent_last, tangent_first = lax.optimization_barrier(
        (
            part_spectrum(to_modes[0], seed_blocks[0], 0),
            heat_state[-1:],
            heat_state[:1],
            tangent_in[-1:],
            tangent_in[:1],
        )
    )

    forward_rhs, tangent_rhs = by_radius(
        rhs_kernel,
        wet_mask,
        [heat_state, *halo_planes(heat_last, heat_first), tangent_in, *halo_planes(tangent_last, tangent_first)],
        [jnp.bfloat16] * 2,
    )
    own_seed, forward_rhs, tangent_rhs = lax.optimization_barrier(
        (seed_blocks[0], forward_rhs, tangent_rhs)
    )
    seed_blocks = [own_seed] + seed_blocks[1:]
    forward_blocks = from_all(forward_rhs)
    tangent_blocks = from_all(tangent_rhs)

    def solve(blocks, formula, first=None):
        returned = []
        for c in range(mode_chunks):
            known = c == 0 and first is not None
            total = first if known else part_spectrum(to_modes[0], blocks[0], c)
            for weights, block in zip(to_modes[1:], blocks[1:]):
                total = total + part_spectrum(weights, block, c)
            solved = jnp.einsum(
                formula, whole[c], total.astype(jnp.bfloat16), preferred_element_type=jnp.float32
            ).astype(jnp.bfloat16)
            returned.append(from_all(solved))
        return returned

    def part_inverse(returned, pairs):
        total = 0.0
        for c, i in pairs:
            total = total + jnp.einsum(
                "ka,kzr->zra",
                to_azimuths[i][c * step : (c + 1) * step],
                returned[c][i],
                preferred_element_type=jnp.float32,
            )
        return total

    pairs = [(c, i) for i in range(size) for c in range(mode_chunks)]

    def inverse(returned):
        return part_inverse(returned, pairs).astype(jnp.bfloat16)

    dual_modes = solve(seed_blocks, "ksr,kzs->kzr", seed_part)
    dual_modes[0][0], *forward_received = lax.optimization_barrier(
        (dual_modes[0][0], *forward_blocks[1:])
    )
    forward_blocks = forward_blocks[:1] + forward_received
    forward_modes = solve(forward_blocks, "krs,kzs->kzr")
    tangent_modes = solve(tangent_blocks, "krs,kzs->kzr")

    dual = inverse(dual_modes)
    (gradient,) = by_radius(
        gradient_kernel, wet_mask, [heat_state, dual, *halo_planes(dual[-1:], dual[:1])], [jnp.float32]
    )

    new_state = inverse(forward_modes)
    radial_index = jnp.arange(radial, dtype=jnp.int32)[None, :, None]
    selected = jnp.where(radial_index == sensors[:, None, :], new_state, jnp.zeros_like(new_state))
    readings = jnp.sum(selected, axis=1)

    partial = part_inverse(tangent_modes, pairs[:-1])
    gradient, partial, tangent_modes[-1][-1] = lax.optimization_barrier(
        (gradient, partial, tangent_modes[-1][-1])
    )
    tangent_out = (partial + part_inverse(tangent_modes, pairs[-1:])).astype(jnp.bfloat16)
    return (new_state, tangent_out, gradient, readings)


fields = 3
parts = 8
early = parts // 2
bounds = (0, 2, 4, 6, 8, 10, 12, 13, 15, 16)
blocks = len(bounds) - 1
sections = ((0, 1, 2), (3, 4, 5), (6, 7, 8))
crossed = (7, 8)
order = (1, 2, 0)
own, other = 0, 1
ticks = 32


def timed(items):
    found = [[] for _ in range(ticks)]
    start = 0
    for item in items:
        found[start // 2].append(item)
        start += bounds[item[0] + 1] - bounds[item[0]]
    return found


def line_order():
    found = []
    for section in sections:
        group = [(q, c) for q in section for c in ((own, other) if q in crossed else (own,))]
        found += [(q, c, p) for p in range(3) for q, c in group]
    return timed(found)


def pair_order():
    found = []
    for section in sections:
        found += [(q, s) for s in range(4) for q in section if q not in crossed]
    found[10:10] = [(q, 0) for q in crossed]
    return timed(found)


def modes_kernel(
    shard, full, cotangent, heat, tangent, wet,
    out_seed, out_forward, out_tangent,
    matrices, table, values, stage, mine, theirs, given, raw, edges, edge_out, edge_in, damp,
    pair_send, pair_recv, up_send, up_recv, down_send, down_recv, azi_send, azi_recv,
    twin_send, twin_recv, back_send, back_recv, keep_sem, load_sem, table_sem, raw_sem, edge_load, edge_send, edge_recv,
):
    outs = (out_seed, out_forward, out_tangent)
    flips = (True, False, False)
    place, azi = lax.axis_index("depth"), lax.axis_index("azi")
    z, x, core = place // 4, place // 2 % 2, place % 2
    pair, twin, up, down = place + 2 - 4 * x, place + 1 - 2 * core, place + 4, place - 4
    count, radial = matrices.shape[1], matrices.shape[3]
    step = count // parts
    fine = count // bounds[-1]
    half = count // 2
    chips = matrices.shape[0]
    slab = mine.shape[2]
    local = heat.shape[2]
    strip = raw.shape[3]
    strips = radial // strip
    last = lax.axis_size("depth") - 1
    planes = slab // parts
    mesh_ids = pl.DeviceIdType.MESH

    barrier = pltpu.get_barrier_semaphore()

    def greet(where, azimuth):
        pl.semaphore_signal(barrier, inc=1, device_id=(where, azimuth), device_id_type=mesh_ids)

    greet(pair, azi)
    greet(twin, azi)
    greet(place, 1 - azi)

    @pl.when(z < 3)
    def _():
        greet(up, azi)

    @pl.when(z > 0)
    def _():
        greet(down, azi)

    @pl.when(place < last)
    def _():
        greet(place + 1, azi)

    @pl.when(place > 0)
    def _():
        greet(place - 1, azi)

    inner = (place + last) // (last + 1) + (2 * last - place) // (last + 1)
    pl.semaphore_wait(barrier, 4 + (z + 1) // 2 % 2 + inner)

    def remote(src, dst, send, recv, where, azimuth=azi):
        return pltpu.make_async_remote_copy(
            src_ref=src, dst_ref=dst, send_sem=send, recv_sem=recv,
            device_id=(where, azimuth), device_id_type=mesh_ids,
        )

    def span_of(q):
        return pl.ds(bounds[q] * fine, (bounds[q + 1] - bounds[q]) * fine)

    def region(q, line, side):
        return matrices.at[2 * line + side, span_of(q)]

    flipped = (z, z + 1 - 2 * (z % 2), z + 2 - 4 * (z // 2), 3 - z)

    def pair_copy(q, s):
        ref = region(q, flipped[s], x)
        return remote(ref, ref, pair_send.at[q, s], pair_recv.at[q, s], pair)

    def line_item(q, c):
        return blocks + crossed.index(q) if c == other else q

    def up_copy(q, c, p):
        ref = region(q, z - p, x if c == own else 1 - x)
        k = line_item(q, c)
        return remote(ref, ref, up_send.at[k, p], up_recv.at[k, p], up)

    def down_copy(q, c, p):
        ref = region(q, z + p, x if c == own else 1 - x)
        k = line_item(q, c)
        return remote(ref, ref, down_send.at[k, p], down_recv.at[k, p], down)

    def azi_copy(n):
        if n < early:
            mine_at = matrices.at[2 * z + x, pl.ds(n * step, step)]
            theirs_at = matrices.at[2 * z + x, pl.ds(half + n * step, step)]
            return remote(mine_at, theirs_at, azi_send.at[n], azi_recv.at[n], place, 1 - azi)
        turn_of, part = divmod(n - early, parts)
        f = order[turn_of]
        span = planes * radial
        at = pl.ds(part * span, span)
        return remote(
            values.at[f, at, pl.ds(0, local)],
            values.at[f, at, pl.ds(local, local)],
            azi_send.at[n], azi_recv.at[n], place, 1 - azi,
        )

    pairs, lines, azis = pair_order(), line_order(), early + fields * parts

    lag, lead = 2, 4

    def each(t, act):
        if 0 <= t < ticks:
            for item in pairs[t]:
                act(pair_copy(*item))

    def azi_until(t):
        return early if t < 2 else min(t + lead + 1, azis)

    def azi_send_up_to(t):
        for n in range(0 if t == 0 else azi_until(t - 1), azi_until(t)):
            azi_copy(n).start()

    def azi_in(begin, end):
        for n in range(begin, end):
            azi_copy(n).wait_recv()

    def send(t):
        each(t, lambda copy: copy.start())
        azi_send_up_to(t)
        for q, c, p in lines[t] if t < ticks else ():

            @pl.when((z < 3) & (z >= p))
            def _():
                up_copy(q, c, p).start()

            @pl.when((z > 0) & (z + p <= 3))
            def _():
                down_copy(q, c, p).start()

    def receive(t):
        if t == early:
            azi_in(0, early)
        each(t, lambda copy: copy.wait_recv())
        for q, c, p in lines[t] if 0 <= t < ticks else ():

            @pl.when(z >= p + 1)
            def _():
                up_copy(q, c, p).wait_recv()

            @pl.when(z + p + 1 <= 3)
            def _():
                down_copy(q, c, p).wait_recv()

    def sent(t):
        each(t, lambda copy: copy.wait_send())
        if t < azis:
            azi_copy(t).wait_send()
        for q, c, p in lines[t]:

            @pl.when((z < 3) & (z >= p))
            def _():
                up_copy(q, c, p).wait_send()

            @pl.when((z > 0) & (z + p <= 3))
            def _():
                down_copy(q, c, p).wait_send()

    shard_load = pltpu.make_async_copy(
        shard, matrices.at[2 * z + x, pl.ds(0, half)], load_sem.at[0]
    )
    shard_load.start()
    damp_load = pltpu.make_async_copy(wet, damp, load_sem.at[1])
    damp_load.start()

    def strip_loads(n):
        slot = n % 2
        c = n % strips
        span = pl.ds(c * strip, strip)
        if n >= strips:
            return [
                pltpu.make_async_copy(
                    cotangent.at[:, span, :], raw.at[slot, 0, pl.ds(1, slab)], raw_sem.at[slot, 0]
                )
            ]
        found = []
        for f, source in enumerate((heat, tangent)):
            found.append((source.at[:, span, :], raw.at[slot, f, pl.ds(1, slab)], 3 * f))
            found.append((edges.at[f, 0, span], raw.at[slot, f, 0], 3 * f + 1))
            found.append((edges.at[f, 1, span], raw.at[slot, f, slab + 1], 3 * f + 2))
        return [pltpu.make_async_copy(a, b, raw_sem.at[slot, i]) for a, b, i in found]

    def edge_copies(side):
        out = []
        for f in range(2):
            out.append(
                remote(
                    edge_out.at[f, side], edge_in.at[f, side],
                    edge_send.at[f, side], edge_recv.at[f, side],
                    place + 1 if side == 0 else place - 1,
                )
            )
        return out

    edge_loads = [
        pltpu.make_async_copy(
            source.at[slab - 1 if side == 0 else 0], edges.at[f, side], edge_load.at[f, side]
        )
        for f, source in enumerate((heat, tangent))
        for side in range(2)
    ]

    def edges_out():
        for load in edge_loads:
            load.start()
        for load in edge_loads:
            load.wait()
        edge_out[...] = edges[...].astype(jnp.bfloat16)

        @pl.when(place < last)
        def _():
            for copy in edge_copies(0):
                copy.start()

        @pl.when(place > 0)
        def _():
            for copy in edge_copies(1):
                copy.start()

    def edges_in():
        for side, empty, full_side in ((0, place == 0, place > 0), (1, place == last, place < last)):

            @pl.when(full_side)
            def _():
                for copy in edge_copies(side):
                    copy.wait_recv()
                edges[:, side] = edge_in[:, side].astype(jnp.float32)

            @pl.when(empty)
            def _():
                edges[:, side] = jnp.zeros((2, radial, local), jnp.float32)

    def edges_sent():
        @pl.when(place < last)
        def _():
            for copy in edge_copies(0):
                copy.wait_send()

        @pl.when(place > 0)
        def _():
            for copy in edge_copies(1):
                copy.wait_send()

    table_loads = []
    for part in range(4):
        owner, which = (azi, 1 - azi)[part % 2], (1 - core, core)[part // 2]
        row = pl.multiple_of((2 * owner + which) * (half), half)
        for h in range(2):
            col = pl.multiple_of((azi, 1 - azi)[h] * local, local)
            table_loads.append(
                pltpu.make_async_copy(
                    full.at[pl.ds(row, half), pl.ds(col, local)],
                    table.at[pl.ds(part * half, half), pl.ds(h * local, local)],
                    table_sem.at[part, h],
                )
            )

    def prepare(n):
        slot = n % 2
        c = n % strips
        if n + 1 < 2 * strips:
            for load in strip_loads(n + 1):
                load.start()
        for load in strip_loads(n):
            load.wait()
        radius = c * strip + lax.broadcasted_iota(jnp.int32, (strip, local), 0)
        profile = evaporation * jnp.exp(-radius.astype(jnp.float32) / skin_depth)

        def plane_step(p, _):
            into = pl.ds(pl.multiple_of(p * radial + c * strip, strip), strip)
            if n >= strips:
                values[0, into, pl.ds(0, local)] = raw[slot, 0, p + 1].astype(jnp.bfloat16)
                return 0
            damping = damp[pl.ds(p, 1), :].astype(jnp.float32) * profile

            def mix(f):
                centre = raw[slot, f, p + 1]
                around = raw[slot, f, p + 2] + raw[slot, f, p]
                return centre, centre + mixing * (around - 2.0 * centre)

            centre, value = mix(0)
            moisture = jnp.tanh(centre)
            values[1, into, pl.ds(0, local)] = (value - damping * moisture).astype(jnp.bfloat16)
            slope = 1.0 - moisture * moisture
            centre, value = mix(1)
            values[2, into, pl.ds(0, local)] = (value - damping * slope * centre).astype(jnp.bfloat16)
            return 0

        lax.fori_loop(0, slab, plane_step, 0)

    def twin_copy(f, part):
        at = pl.ds(part * half, half)
        return remote(
            given.at[order.index(f) % 2, at], theirs.at[f, at], twin_send.at[f, part], twin_recv.at[f, part], twin
        )

    group = 4

    def transform(f, n):
        span = group * radial
        cols = values[f, pl.ds(n * span, span), :]

        def half_step(h, _):
            weights = table[pl.ds(pl.multiple_of(h * count, count), count), :]
            out = lax.dot_general(
                weights, cols, (((1,), (1,)), ((), ())), preferred_element_type=jnp.float32
            )
            for g in range(group):
                at = pl.multiple_of((n * group + g) * 2 * count + h * count, count)
                stage[pl.ds(at, count), :] = out[:, g * radial : (g + 1) * radial]
            return 0

        lax.fori_loop(0, 2, half_step, 0)

    def turn(into, f, first, begin, end):
        def one(n, _):
            for u in range(8):
                k = n * 8 + u
                into[f, k] = stage[pl.ds(first + k, slab, stride=2 * count), :].astype(jnp.bfloat16)
            return 0

        lax.fori_loop(begin // 8, end // 8, one, 0)

    def give(f):
        for part in range(2):
            if f == order[2]:
                twin_copy(order[0], part).wait_send()
            turn(given, order.index(f) % 2, 0, part * half, (part + 1) * half)
            twin_copy(f, part).start()

    def take(f):
        turn(mine, f, count, 0, count)

    def keep_copy(f, q):
        at = span_of(q)
        return pltpu.make_async_copy(mine.at[f, at], outs[f].at[at], keep_sem.at[f, q])

    def back_copy(f, q):
        return remote(
            theirs.at[f, span_of(q)],
            outs[f].at[pl.ds(count + bounds[q] * fine, (bounds[q + 1] - bounds[q]) * fine)],
            back_send.at[f, q], back_recv.at[f, q], twin,
        )

    def solve(which, q):
        def one(n, _):
            found = []
            for u in range(32):
                k = bounds[q] * fine + n * 32 + u
                matrix = jnp.concatenate([matrices[c, k] for c in range(chips)], axis=0)
                for flip in (True, False):
                    chosen = [f for f in which if flips[f] == flip]
                    if not chosen:
                        continue
                    stacked = jnp.concatenate(
                        [part[f, k] for f in chosen for part in (mine, theirs)], axis=0
                    )
                    out = lax.dot_general(
                        stacked, matrix, (((1,), (0 if flip else 1,)), ((), ())),
                        preferred_element_type=jnp.float32,
                    )
                    found.append((chosen, k, out))
            for chosen, k, out in found:
                out = out.astype(jnp.bfloat16)
                for i, f in enumerate(chosen):
                    mine[f, k] = out[2 * i * slab : (2 * i + 1) * slab]
                    theirs[f, k] = out[(2 * i + 1) * slab : (2 * i + 2) * slab]
            return 0

        lax.fori_loop(0, (bounds[q + 1] - bounds[q]) * fine // 32, one, 0)
        for f in which:
            keep_copy(f, q).start()
            back_copy(f, q).start()

    def met(f, part):
        twin_copy(f, part).wait_recv()

    def begin():
        edges_out()
        for load in table_loads:
            load.start()
        damp_load.wait()
        edges_in()
        for load in strip_loads(0):
            load.start()
        for n in range(4):
            prepare(n)

    def table_in():
        for load in table_loads:
            load.wait()

    P = functools.partial
    tasks = {
        0: [begin],
        1: [P(prepare, n) for n in range(4, strips)],
        2: [P(prepare, n) for n in range(strips, strips + 4)],
        4: [P(prepare, n) for n in range(strips + 4, 2 * strips)],
        3: [table_in],
    }
    for turn_of, f in enumerate(order):
        for n in range(slab // group):
            begin = early + turn_of * parts + n * group // planes
            end = begin + group // planes
            ready = end - (2 if turn_of == 2 else 1)
            tasks.setdefault(ready, []).append(P(azi_in, begin, end))
            tasks[ready].append(P(transform, f, n))
    more = {
        11: [P(give, 1), P(take, 1)],
        13: [P(met, 1, 0), P(met, 1, 1), P(solve, [1], 0)],
        14: [P(solve, [1], 1)],
        15: [P(solve, [1], 2)],
        19: [P(give, 2), P(take, 2)],
        21: [P(met, 2, 0), P(met, 2, 1), P(solve, [2], 0)],
        22: [P(solve, [2], 1), P(solve, [2], 2)],
        24: [P(solve, [1, 2], 3)],
        25: [P(solve, [1, 2], 4)],
        26: [P(give, 0), P(take, 0), P(solve, [1, 2], 5)],
        27: [P(met, 0, 0)] + [P(solve, [0], q) for q in range(4)],
        28: [P(solve, [1, 2], 7), P(met, 0, 1)] + [P(solve, [0], q) for q in (4, 5, 7)],
        29: [P(solve, [0, 1, 2], 6)],
        30: [P(solve, [0, 1, 2], 8)],
    }
    for t, found in more.items():
        tasks.setdefault(t, []).extend(found)

    shard_load.wait()
    for t in range(ticks - 1):
        receive(t - lag)
        send(t)
        for task in tasks.get(t, []):
            task()

    edges_sent()
    for t in range(ticks - 1):
        sent(t)
    for f in range(fields):
        for part in range(2):
            if f != order[0]:
                twin_copy(f, part).wait_send()
        for q in range(blocks):
            keep_copy(f, q).wait()
            back_copy(f, q).wait()


def solved_modes(shard, table, cotangent, heat, tangent, wet):
    slab, radial, local = heat.shape
    half, rows, _ = shard.shape
    count = 2 * half
    strip = 16
    dma = pltpu.SemaphoreType.DMA
    out = jax.ShapeDtypeStruct((2 * count, slab, radial), jnp.bfloat16)
    modes = pltpu.VMEM((fields, count, slab, radial), jnp.bfloat16)
    return pl.pallas_call(
        modes_kernel,
        out_shape=[out] * fields,
        in_specs=[pl.BlockSpec(memory_space=pl.ANY)] * 6,
        out_specs=[pl.BlockSpec(memory_space=pl.ANY)] * fields,
        scratch_shapes=[
            pltpu.VMEM((radial // rows, count, rows, radial), jnp.bfloat16),
            pltpu.VMEM((2 * count, 2 * local), jnp.bfloat16),
            pltpu.VMEM((fields, slab * radial, 2 * local), jnp.bfloat16),
            pltpu.VMEM((2 * slab * count, radial), jnp.float32),
            modes,
            modes,
            pltpu.VMEM((2, count, slab, radial), jnp.bfloat16),
            pltpu.VMEM((2, 2, slab + 2, strip, local), jnp.float32),
            pltpu.VMEM((2, 2, radial, local), jnp.float32),
            pltpu.VMEM((2, 2, radial, local), jnp.bfloat16),
            pltpu.VMEM((2, 2, radial, local), jnp.bfloat16),
            pltpu.VMEM((slab, local), jnp.int32),
            dma((blocks, 4)), dma((blocks, 4)),
            dma((blocks + len(crossed), 3)), dma((blocks + len(crossed), 3)),
            dma((blocks + len(crossed), 3)), dma((blocks + len(crossed), 3)),
            dma((early + fields * parts,)), dma((early + fields * parts,)),
            dma((fields, 2)), dma((fields, 2)),
            dma((fields, blocks)), dma((fields, blocks)), dma((fields, blocks)),
            dma((2,)), dma((4, 2)), dma((2, 6)), dma((2, 2)), dma((2, 2)), dma((2, 2)),
        ],
        compiler_params=pltpu.CompilerParams(
            collective_id=0, has_side_effects=True, vmem_limit_bytes=62 * 1024 * 1024
        ),
        cost_estimate=pl.CostEstimate(flops=15 * 10**9, bytes_accessed=10**8, transcendentals=0),
    )(shard, table, cotangent, heat, tangent, wet)


def edged_gradient_kernel(wet, heat, dual, before, after, out):
    rows = heat.shape[1]
    at = pl.ds(pl.multiple_of(pl.program_id(0) * rows, rows), rows)
    gradient_kernel(wet, heat, dual, before.at[:, at], after.at[:, at], out)


def edged_gradient(wet, heat, dual, before, after):
    slab, radial, lanes = heat.shape
    rows = 32
    spec = pl.BlockSpec((slab, rows, lanes), lambda i: (0, i, 0))
    whole = pl.BlockSpec(memory_space=pltpu.VMEM)
    return pl.pallas_call(
        edged_gradient_kernel,
        grid=(radial // rows,),
        in_specs=[whole, spec, spec, whole, whole],
        out_specs=spec,
        out_shape=jax.ShapeDtypeStruct(heat.shape, jnp.float32),
        cost_estimate=pl.CostEstimate(
            flops=10 * heat.size, bytes_accessed=10 * heat.size, transcendentals=heat.size
        ),
    )(wet, heat, dual, before, after)


def fused_body(table, heat_state, tangent_in, cotangent, wet_mask, sensors, propagators):
    slab, radial, local_azi = heat_state.shape
    depth = lax.axis_size("depth")
    me = lax.axis_index("azi")
    core = lax.rem(lax.axis_index("depth"), 2)
    modes = propagators.shape[0]
    half = modes // 2

    mine = lax.dynamic_slice_in_dim(propagators, core * half, half, axis=0)
    outgoing = lax.dynamic_slice_in_dim(propagators, (1 - core) * half, half, axis=0)
    incoming = lax.ppermute(outgoing, "depth", [(i, i ^ 1) for i in range(depth)])
    rows = mine.shape[1]
    at_core = lax.broadcasted_iota(jnp.int32, (1, 2, 1, 1), 1) == core
    shard = jnp.where(at_core, mine[:, None], incoming[:, None]).reshape(half, 2 * rows, radial)

    def table_rows(which):
        return [
            lax.dynamic_slice_in_dim(table, owner * modes + which * half, half, axis=0)
            for owner in (me, 1 - me)
        ]

    own_rows = jnp.concatenate(table_rows(core), axis=0)
    twin_rows = jnp.concatenate(table_rows(1 - core), axis=0)

    def columns(weights, owner):
        return lax.dynamic_slice_in_dim(weights, owner * local_azi, local_azi, axis=1)

    to_azimuths = columns(jnp.concatenate([own_rows, twin_rows], axis=0), me)

    dual_modes, forward_modes, tangent_modes = solved_modes(
        shard, table, cotangent, heat_state, tangent_in, wet_mask
    )

    def inverse(solved):
        return jnp.einsum(
            "ka,kzr->zra", to_azimuths, solved, preferred_element_type=jnp.float32
        ).astype(jnp.bfloat16)

    dual = inverse(dual_modes)
    gradient = edged_gradient(wet_mask, heat_state, dual, *halo_planes(dual[-1:], dual[:1]))
    new_state = inverse(forward_modes)
    radial_index = jnp.arange(radial, dtype=jnp.int32)[None, :, None]
    selected = jnp.where(radial_index == sensors[:, None, :], new_state, jnp.zeros_like(new_state))
    readings = jnp.sum(selected, axis=1)
    tangent_out = inverse(tangent_modes)
    return (new_state, tangent_out, gradient, readings)


def solution(mesh):
    def run(heat_state, tangent_in, cotangent, wet_mask, sensors, propagators):
        table = jnp.asarray(fourier_table(heat_state.shape[2]))
        field = P("depth", None, "azi")
        fits = mesh.shape["azi"] == 2 and mesh.shape["depth"] == 16
        body = fused_body if fits else split_body
        panel = P("depth", "azi")
        return jax.shard_map(
            body,
            mesh=mesh,
            in_specs=(P(), field, field, field, panel, panel, P("azi", "depth", None)),
            out_specs=(field, field, field, panel),
            check_vma=False,
        )(table, heat_state, tangent_in, cotangent, wet_mask, sensors, propagators)

    return run
```
